32 devices in a mesh: groups: 2 (over x), gx: 16 (over z, y, core).
Axes of the slice: x: 2, y: 2, z: 4, core: 2. Of those that a mesh axis runs over, the one named last changes fastest.
Arguments:
- fracture: float32 [2, 64, 4, 128], P(None, ('groups', 'gx')), parts along dimension 1, may hold values from -6 to 6
- cell_class: int32 [64, 4, 128], P(('groups', 'gx')), parts along dimension 0, may hold values from 0 to 1
- owner: int32 [64, 4, 128, 1], P(('groups', 'gx')), parts along dimension 0, may hold values from 0 to 15; in each aligned block of 1024 rows (0 to 1023, 1024 to 2047, ..., all dimensions but the last counted through in order) at most 80 rows name the same one
- matrix: float32 [128, 2, 40960], P(None, None, ('groups', 'gx')), parts along dimension 2, may hold values from -6 to 6
- velocity: float32 [2, 3], replicated, may hold values from -0.3 to 0.3
- coupling: float32 [2], replicated, may hold values from 0.2 to 0.6
- operators: float32 [2, 128, 128], replicated, may hold values from -1 to 1
Outputs:
- age_moments: float32 [2, 64, 4, 128], P(None, ('groups', 'gx')), parts along dimension 1
- matrix_moments: float32 [128, 2, 40960], P(None, None, ('groups', 'gx')), parts along dimension 2
The draws below stay inside these ranges and needn't reach their ends.
There are 2 independent parts, one for each index of `groups`. The reference program is written for one: setup_inputs(seed, part) draws one part's arguments, and reference() takes and returns one part's arrays. A program takes and returns all parts, laid end to end along the dimension named above; an argument that names none is the same for every part. Nothing has to cross between parts.
Inputs may be any that keep to these rules, and one draw needn't show every extreme that they name: Among the cells of one index of gx, at most 80 have the same owner, and some owner takes exactly 80 of them.
All inputs are finite; a program needn't handle non-finite values.
Results may differ from the reference program's by a relative error of at most 0.0001.
Values sent between devices are 32-bit elements; how exact they have to be, the bound alone decides.
A program may use at most 64 MiB of HBM per device.

```python
import math
import jax
import jax.numpy as jnp
import numpy as np
from jax import lax

M = 128
NCLS = 2
CX = 2
NY = 4
NZ = 128
STEPS = 8
SUBSTEPS = 2
SLOTS = 1280
CAP = 80
NX = 32
COLS = 20480
N_GX = 16


def draw_operators(key, part):
    diagonal_key, spread_key = jax.random.split(jax.random.fold_in(key, 7))
    diagonal = jax.random.uniform(diagonal_key, (NCLS, M), jnp.float32, 0.4, 0.8)
    spread = jnp.clip(jax.random.normal(spread_key, (NCLS, M, M), jnp.float32), -4.0, 4.0) * (0.2 / math.sqrt(M))
    identity = jnp.eye(M, dtype=jnp.float32)
    return spread * (1.0 - identity)[None, :, :] + diagonal[:, :, None] * identity[None, :, :]


def set_ends(result, rng, least, largest):
    extent = result.shape
    place = [jax.random.randint(jax.random.fold_in(rng, axis), (), 0, extent[axis]) for axis in range(len(extent))]
    result = result.at[tuple(place)].set(least)
    longest = extent.index(max(extent))
    place[longest] = (place[longest] + 1) % extent[longest]
    return result.at[tuple(place)].set(largest)


def block_scale(rng, extent, shards, least, largest):
    loudness, own = 1.0, jax.random.fold_in(rng, 6)
    for axis_at, parts in shards:
        steps = jnp.exp(jax.random.uniform(jax.random.fold_in(own, axis_at), (parts,), jnp.float32, least / len(shards), largest / len(shards)))
        loudness = loudness * jnp.repeat(steps, extent[axis_at] // parts).reshape([-1 if axis == axis_at else 1 for axis in range(len(extent))])
    return loudness


def shared_out(key, own, number, rows, number_of, top, reach, slope):
    order = jax.random.permutation(key, number_of)
    heavy_load, common = load_shares(number_of, rows * top, reach, slope, True), load_shares(number_of, rows * top, reach, slope, False)
    places = jnp.arange(number_of)

    def named(sizes, turn):
        used = int((sizes > 0).sum())
        fixed = max(1, used // 4)
        passed = fixed + (places - fixed + turn * (used - fixed)) % max(1, number_of - fixed)
        return jnp.zeros((number_of,), jnp.int32).at[order[jnp.where(places < fixed, places, passed)]].set(jnp.asarray(sizes, jnp.int32))

    sizes = jnp.where(number % 4 == 0, named(heavy_load, number // 4), named(common, number - number // 4 - 1))
    mixed = jax.random.permutation(jax.random.fold_in(own, 3), number_of)
    source_of, taker = mixed[0:number_of // 2 * 2:2], mixed[1:number_of // 2 * 2:2]
    margin = jnp.minimum(sizes[source_of] - 1, reach - sizes[taker]) // 2
    margin = jnp.where((source_of == order[0]) | (taker == order[0]) | (sizes[taker] == 0), 0, jnp.maximum(margin, 0))
    passed = jax.random.randint(jax.random.fold_in(own, 4), (number_of // 2,), 0, 1 << 20) % (margin + 1)
    sizes = sizes.at[source_of].add(-passed).at[taker].add(passed)
    members = jnp.searchsorted(jnp.cumsum(sizes), jnp.arange(rows * top), side="right").astype(jnp.int32)
    table = members.reshape(top, rows).T
    table = table[jax.random.permutation(jax.random.fold_in(own, 1), rows)]
    turn = jax.random.randint(jax.random.fold_in(own, 2), (rows, 1), 0, top)
    return jnp.take_along_axis(table, (jnp.arange(top)[None, :] + turn) % top, axis=1)


def load_shares(number_of, total, bound, lean, full):
    weights = [(1 << 20) // math.isqrt(rank ** lean) + 1 for rank in range(1, number_of + 1)]
    largest = bound if full else min(bound, max(-(-total // number_of), total * weights[0] // sum(weights)))
    least = 1 if total - largest >= number_of - 1 else 0
    counts, surplus = [largest] + [least] * (number_of - 1), total - largest - least * (number_of - 1)
    while surplus > 0:
        free = [i for i in range(1, number_of) if counts[i] < largest] or [i for i in range(1, number_of) if counts[i] < bound]
        whole, left = sum([weights[i] for i in free]), surplus
        for i in free:
            more = min(bound - counts[i], max(1, left * weights[i] // whole), surplus)
            counts[i] = counts[i] + more
            surplus = surplus - more
    return np.array(counts)


def bell_draw(own_key, shape, width, limit, cuts=(), held_as=jnp.bfloat16):
    values = width * jax.random.normal(own_key, shape, jnp.float32)
    if cuts:
        values = values * block_scale(own_key, shape, cuts, -0.22, 0.18)
    return jnp.clip(values, -limit, limit).astype(held_as)


def setup_inputs(seed: int = 0, part: int = 0) -> dict:
    splits = jax.random.split(jax.random.key(seed), 8)
    own_keys = jax.random.split(jax.random.fold_in(splits[7], part), 8)
    fracture = bell_draw(own_keys[0], (2, NX, NY, NZ), 1.0, 6.0, ((1, 16),), jnp.float32)
    cell_class = set_ends(jax.random.randint(own_keys[1], (NX, NY, NZ), 0, NCLS), jax.random.fold_in(own_keys[1], 1), 0, NCLS - 1).astype(jnp.int32)
    owner_keys = jax.random.split(jax.random.fold_in(own_keys[2], 1), NX * NY * NZ // (CX * NY * NZ))
    owner_turns = jax.random.permutation(jax.random.fold_in(own_keys[2], 3), NX * NY * NZ // (CX * NY * NZ))
    owner = jax.vmap(lambda own, number: shared_out(jax.random.fold_in(own_keys[2], 2), own, number, CX * NY * NZ, N_GX, 1, CAP, 2))(owner_keys, owner_turns).reshape((NX, NY, NZ, 1))
    matrix = bell_draw(own_keys[3], (M, 2, COLS), 1.0, 6.0, ((2, 16),), jnp.float32)
    velocity = jnp.clip(jax.random.uniform(splits[4], (NCLS, 3), jnp.float32, -0.3, 0.3), -0.3, 0.3)
    coupling = jnp.clip(jax.random.uniform(splits[5], (NCLS,), jnp.float32, 0.2, 0.6), 0.2, 0.6)
    operators = draw_operators(jax.random.fold_in(splits[7], 71), part)
    return dict(fracture=fracture, cell_class=cell_class, owner=owner, matrix=matrix, velocity=velocity, coupling=coupling, operators=operators)


TIME_STEP = 0.125


def advect(moments, flow_speed):
    padded = jnp.pad(moments, ((0, 0), (1, 1), (1, 1), (1, 1)))
    center = padded[:, 1:-1, 1:-1, 1:-1]
    lower_side = (padded[:, :-2, 1:-1, 1:-1], padded[:, 1:-1, :-2, 1:-1], padded[:, 1:-1, 1:-1, :-2])
    upper_side = (padded[:, 2:, 1:-1, 1:-1], padded[:, 1:-1, 2:, 1:-1], padded[:, 1:-1, 1:-1, 2:])
    change = jnp.zeros_like(moments)
    for direction in range(3):
        forward = jnp.maximum(flow_speed[direction], 0.0)
        backward = jnp.minimum(flow_speed[direction], 0.0)
        change = change + forward * (center - lower_side[direction]) + backward * (upper_side[direction] - center)
    return center - change


def reference(fracture, cell_class, owner, matrix, velocity, coupling, operators):
    cell_count = CX * NY * NZ
    owner_flat = owner.reshape(N_GX, cell_count)
    owner_onehot = (owner_flat[:, :, None] == jnp.arange(N_GX, dtype=jnp.int32)[None, None, :]).astype(jnp.int32)
    arrival = jnp.sum((jnp.cumsum(owner_onehot, axis=1) - 1) * owner_onehot, axis=2)
    source_index = jnp.arange(N_GX, dtype=jnp.int32)[:, None]
    slot = (owner_flat * SLOTS + source_index * CAP + arrival).reshape(-1).astype(jnp.int32)
    column_class = jnp.zeros((COLS,), jnp.int32).at[slot].set(cell_class.reshape(-1))
    speed_rows = []
    for direction in range(3):
        speed_now = jnp.zeros(cell_class.shape, jnp.float32)
        for class_id in range(NCLS):
            speed_now = speed_now + jnp.where(cell_class == class_id, velocity[class_id, direction], 0.0)
        speed_rows.append(speed_now)
    flow_speed = jnp.stack(speed_rows)
    column_coupling = jnp.zeros((COLS,), jnp.float32)
    for class_id in range(NCLS):
        column_coupling = column_coupling + jnp.where(column_class == class_id, coupling[class_id], 0.0)
    moments = fracture
    column_state = matrix
    for step_index in range(STEPS):
        for substep in range(SUBSTEPS):
            moments = advect(moments, flow_speed)
        moments = jnp.stack([moments[0] + TIME_STEP, moments[1] + 2.0 * TIME_STEP * moments[0]])
        column_values = jnp.zeros((2, COLS), jnp.float32).at[:, slot].set(moments.reshape(2, -1))
        right_side = jnp.stack([column_state[:, 0] + TIME_STEP, column_state[:, 1] + 2.0 * TIME_STEP * column_state[:, 0]], axis=1)
        right_side = right_side.at[0].add(column_coupling[None, :] * column_values)
        flat_side = right_side.reshape(M, 2 * COLS)
        updated = jnp.zeros((M, 2, COLS), jnp.float32)
        for class_id in range(NCLS):
            product = jnp.dot(operators[class_id], flat_side, precision=lax.Precision.HIGHEST)
            updated = jnp.where((column_class == class_id)[None, None, :], product.reshape(M, 2, COLS), updated)
        column_state = updated
        fluxes = column_coupling[None, :] * (column_state[0] - column_values)
        moments = moments + fluxes[:, slot].reshape(moments.shape)
    return moments, column_state
```

```python
import functools

import jax
import jax.numpy as jnp
from jax import lax
from jax.experimental import pallas as pl
from jax.experimental.pallas import tpu as pltpu
from jax.sharding import PartitionSpec as P

STEPS = 8
SUBSTEPS = 2
TIME_STEP = 0.125
MEAN_RATE = 2.0 * TIME_STEP
BLOCK = 4
LANES = 128
HALF = STEPS // 2

F32 = jnp.float32
BF16 = jnp.bfloat16
NN = (((1,), (0,)), ((), ()))
NT = (((1,), (1,)), ((), ()))


def full_dot(a, b, dims=NN):
    return lax.dot_general(a, b, dims, precision=lax.Precision.HIGHEST, preferred_element_type=F32)


def half_dot(a, b, dims=NN):
    return lax.dot_general(a, b, dims, preferred_element_type=F32)


def two_parts(x):
    high = x.astype(BF16)
    low = (x - high.astype(F32)).astype(BF16)
    return high, low


def iota(shape, dim):
    return lax.broadcasted_iota(jnp.int32, shape, dim)


def roll_rows(x, shift):
    return pltpu.roll(x, shift, x.ndim - 2)


def roll_lanes(x, shift):
    shift = shift % LANES
    return x if shift == 0 else pltpu.roll(x, shift, x.ndim - 1)


def kernel(
    n,
    cap,
    kinds,
    chunks,
    frac,
    cls,
    own,
    mat,
    vel,
    coup,
    ops,
    age_out,
    mat_out,
    hot,
    mat_v,
    s_hi,
    s_lo,
    main,
    rows_pow,
    cols_pow,
    cols_t,
    fields,
    cls_send,
    cls_recv,
    tile_send,
    tile_recv,
    h0_send,
    h0_recv,
    h1_send,
    h1_recv,
    h2_send,
    h2_recv,
    mat_sem,
    a_send_sem,
    a_recv_sem,
    h_send_sem,
    h_recv_sem,
):
    me = lax.axis_index("gx")
    row8 = iota((8, LANES), 0)
    lane8 = iota((8, LANES), 1)

    load = pltpu.make_async_copy(mat, mat_v, mat_sem)
    load.start()

    sides = ((0, -1), (1, 1))
    for d in range(1, BLOCK + 1):
        for side, sign in sides:
            source = me + sign * d

            @pl.when((source < 0) | (source >= n))
            def _():
                h0_recv[side, d - 1] = jnp.zeros(h0_recv.shape[2:], F32)
                h2_recv[side, d - 1] = jnp.zeros(h2_recv.shape[2:], F32)
                if d < BLOCK:
                    h1_recv[side, d - 1] = jnp.zeros(h1_recv.shape[2:], F32)

    barrier = pltpu.get_barrier_semaphore()

    @pl.loop(1, n)
    def _(d):
        pl.semaphore_signal(
            barrier,
            inc=1,
            device_id={"gx": lax.rem(me + d, n)},
            device_id_type=pl.DeviceIdType.MESH,
        )

    def exchange(send, recv, which, d, peer, landing):
        return pltpu.make_async_remote_copy(
            src_ref=send.at[peer],
            dst_ref=recv.at[landing],
            send_sem=a_send_sem.at[which, d],
            recv_sem=a_recv_sem.at[which, landing],
            device_id={"gx": peer},
            device_id_type=pl.DeviceIdType.MESH,
        )

    def exchange_start(send, recv, which):
        @pl.loop(1, n)
        def _(d):
            exchange(send, recv, which, d, lax.rem(me + d, n), me).start()

        recv[me] = send[me]

    def exchange_arrived(send, recv, which):
        @pl.loop(1, n)
        def _(d):
            source = lax.rem(me + n - d, n)
            exchange(send, recv, which, d, source, source).wait_recv()

    def exchange_sent(send, recv, which):
        @pl.loop(1, n)
        def _(d):
            exchange(send, recv, which, d, lax.rem(me + d, n), me).wait_send()

    def halo(send, recv, which, d, side, sign, rows):
        return pltpu.make_async_remote_copy(
            src_ref=send.at[pl.ds(0, rows)],
            dst_ref=recv.at[side, d - 1, pl.ds(0, rows)],
            send_sem=h_send_sem.at[which, side, d - 1],
            recv_sem=h_recv_sem.at[which, side, d - 1],
            device_id={"gx": me - sign * d},
            device_id_type=pl.DeviceIdType.MESH,
        )

    def halo_each(send, recv, which, reach, rows_of, what):
        for d in range(1, reach + 1):
            for side, sign in sides:
                peer = me + sign * d if what == "arrived" else me - sign * d

                @pl.when((peer >= 0) & (peer < n))
                def _():
                    copy = halo(send, recv, which, d, side, sign, rows_of(d))
                    if what == "start":
                        copy.start()
                    elif what == "arrived":
                        copy.wait_recv()
                    else:
                        copy.wait_send()

    owner_f = own[...].astype(F32)
    class_f = cls[...].astype(F32)
    owner_row = iota((n, LANES), 0).astype(F32)
    named = [jnp.where(owner_row == owner_f[r : r + 1, :], 1.0, 0.0) for r in range(8)]
    named_all = jnp.concatenate(named, axis=0).astype(BF16)
    earlier = jnp.where(iota((LANES, LANES), 0) < iota((LANES, LANES), 1), 1.0, 0.0).astype(BF16)
    before = half_dot(named_all, earlier)
    total = half_dot(named_all, jnp.ones((LANES, LANES), BF16))
    base = jnp.zeros((n, LANES), F32)
    places = []
    for r in range(8):
        count = before[r * n : (r + 1) * n] + base
        base = base + total[r * n : (r + 1) * n]
        arrival = jnp.sum(named[r] * count, axis=0, keepdims=True)
        places.append(owner_f[r : r + 1, :] * float(LANES) + arrival)
    slot_row = iota((LANES, LANES), 0).astype(F32)

    @pl.loop(0, n)
    def _(e):
        start = pl.multiple_of(e * LANES, LANES)
        shift = (e * LANES).astype(F32)
        for r in range(8):
            hit = slot_row == (places[r] - shift)
            hot[pl.ds(start, LANES), r * LANES : (r + 1) * LANES] = jnp.where(hit, 1.0, 0.0).astype(
                BF16
            )

    class_rows = jnp.concatenate(
        [jnp.broadcast_to(class_f[r : r + 1, :], (16, LANES)) for r in range(8)], axis=1
    ).astype(BF16)
    class_out = half_dot(class_rows, hot[...], NT)
    for e in range(n):
        cls_send[e] = class_out[0:1, e * LANES : (e + 1) * LANES]
    h0_send[0] = frac[0]
    h0_send[1] = frac[1]
    h0_send[2] = class_f

    pl.semaphore_wait(barrier, n - 1)
    exchange_start(cls_send, cls_recv, 0)
    halo_each(h0_send, h0_recv, 0, BLOCK, lambda d: 3, "start")

    rows_pow[...] = jnp.zeros(rows_pow.shape, F32)
    squares, fourths = [], []
    for k in range(kinds):
        first = ops[k]
        square = full_dot(first, first)
        fourth = full_dot(square, square)
        squares.append(square)
        fourths.append(fourth)
        at = k * STEPS
        rows_pow[at : at + 1] = first[0:1]
        rows_pow[at + 1 : at + 2] = square[0:1]
        rows_pow[at + 2 : at + 4] = full_dot(rows_pow[at : at + 8], square)[0:2]
        rows_pow[at + 4 : at + 8] = full_dot(rows_pow[at : at + 8], fourth)[0:4]

    load.wait()
    stride = 2 * chunks
    for m in range(2):
        for c in range(chunks):
            at = (m * chunks + c) * LANES
            block = mat_v[pl.ds(c * 2 + m, LANES, stride=stride), :]
            high, low = two_parts(block)
            s_hi[:, at : at + LANES] = high
            s_lo[:, at : at + LANES] = low

    powers = rows_pow[...]
    p_high, p_low = two_parts(powers)
    wide = half_dot(jnp.concatenate([p_high, p_low], axis=0), s_hi[...])
    count = kinds * STEPS
    q_all = wide[:count] + wide[count:] + half_dot(p_high, s_lo[...])

    exchange_arrived(cls_send, cls_recv, 0)
    rolled_lane = lane8

    def to_columns(blocks):
        out = [jnp.zeros((8, LANES), F32) for _ in range(chunks)]
        for s in range(n):
            at, off = divmod(s * cap, LANES)
            turned = roll_lanes(blocks[s], off)
            if off + cap <= LANES:
                out[at] = out[at] + turned
            else:
                out[at] = out[at] + jnp.where(rolled_lane >= off, turned, 0.0)
                out[at + 1] = out[at + 1] + jnp.where(rolled_lane < off, turned, 0.0)
        return out

    def from_columns(columns):
        out = []
        for s in range(n):
            at, off = divmod(s * cap, LANES)
            block = roll_lanes(columns[at], -off)
            if off + cap > LANES:
                block = jnp.where(
                    rolled_lane < LANES - off, block, roll_lanes(columns[at + 1], -off)
                )
            out.append(jnp.where(rolled_lane < cap, block, 0.0))
        return out

    column_class = to_columns([jnp.broadcast_to(cls_recv[s], (8, LANES)) for s in range(n)])

    steady0, steady1 = [], []
    for k in range(kinds):
        sums = jnp.sum(powers[k * STEPS : (k + 1) * STEPS], axis=1, keepdims=True)
        sums = jnp.broadcast_to(sums, (STEPS, LANES))
        zero_sum = jnp.zeros((STEPS, LANES), F32)
        one_sum = jnp.zeros((STEPS, LANES), F32)
        for i in range(STEPS):
            term = jnp.where(row8 >= i, sums[i : i + 1], 0.0)
            zero_sum = zero_sum + TIME_STEP * term
            one_sum = one_sum + (TIME_STEP * MEAN_RATE * i) * term
        steady0.append(zero_sum)
        steady1.append(one_sum)

    def pick(options, which):
        value = options[0]
        for k in range(1, kinds):
            value = jnp.where(which == float(k), options[k], value)
        return value

    step_row = (row8 + 1).astype(F32)
    tiles_a, tiles_b = [], []
    for c in range(chunks):
        parts = []
        for m in range(2):
            at = (m * chunks + c) * LANES
            parts.append(
                pick(
                    [q_all[k * STEPS : (k + 1) * STEPS, at : at + LANES] for k in range(kinds)],
                    column_class[c],
                )
            )
        free0 = parts[0] + pick(steady0, column_class[c])
        free1 = parts[1] + MEAN_RATE * step_row * parts[0] + pick(steady1, column_class[c])
        tiles_a.append(jnp.where(row8 < HALF, free0, roll_rows(free1, HALF)))
        tiles_b.append(jnp.where(row8 < HALF, roll_rows(free0, HALF), free1))
    for half, tiles in ((0, tiles_a), (1, tiles_b)):
        blocks = from_columns(tiles)
        for e in range(n):
            tile_send[half, e] = blocks[e]
        exchange_start(tile_send.at[half], tile_recv.at[half], 1 + half)

    eights = [full_dot(fourths[k], fourths[k]) for k in range(kinds)]
    e_high, e_low = two_parts(jnp.concatenate(eights, axis=0))
    nodes = eights[0].shape[0]
    for b in range(chunks):
        lanes = slice(b * 2 * LANES, (b + 1) * 2 * LANES)
        right = s_hi[:, lanes]
        both = half_dot(e_high, right) + half_dot(e_low, right) + half_dot(e_high, s_lo[:, lanes])
        for i in range(2):
            at = b * 2 + i
            which = column_class[at % chunks][0:1]
            main[:, at * LANES : (at + 1) * LANES] = pick(
                [
                    both[k * nodes : (k + 1) * nodes, i * LANES : (i + 1) * LANES]
                    for k in range(kinds)
                ],
                which,
            )

    wide_rows = kinds * 16
    cols_t[...] = jnp.zeros(cols_t.shape, F32)
    for k in range(kinds):
        turned = ops[k].T
        cols_pow[...] = jnp.zeros(cols_pow.shape, F32)
        cols_pow[0:1] = turned[0:1]
        cols_pow[1:2] = jnp.sum(turned, axis=0, keepdims=True)
        cols_pow[2:4] = full_dot(cols_pow[0:8], ops[k], NT)[0:2]
        cols_pow[4:8] = full_dot(cols_pow[0:8], squares[k], NT)[0:4]
        cols_pow[8:16] = full_dot(cols_pow[0:8], fourths[k], NT)
        zero_sum = jnp.zeros((1, LANES), F32)
        one_sum = jnp.zeros((1, LANES), F32)
        for i in range(STEPS):
            cols_t[k * 16 + 7 - i : k * 16 + 8 - i] = cols_pow[2 * i : 2 * i + 1]
            source_row = cols_pow[2 * i + 1 : 2 * i + 2]
            zero_sum = zero_sum + TIME_STEP * source_row
            one_sum = one_sum + (TIME_STEP * MEAN_RATE * i) * source_row
        cols_t[k * 16 + 8 : k * 16 + 9] = zero_sum
        cols_t[k * 16 + 9 : k * 16 + 10] = one_sum
    whole = cols_t[0:wide_rows]
    whole_high = whole.astype(BF16).astype(F32)
    cols_t[0:wide_rows] = whole_high
    cols_t[wide_rows : 2 * wide_rows] = whole_high
    cols_t[2 * wide_rows : 3 * wide_rows] = whole - whole_high
    response = cols_t[...].T.astype(BF16)

    halo_each(h0_send, h0_recv, 0, BLOCK, lambda d: 3, "arrived")

    def window(recv, index, own_value, reach):
        left = [recv[0, d - 1, index] for d in range(reach, 0, -1)]
        right = [recv[1, d - 1, index] for d in range(1, reach + 1)]
        return jnp.stack(left + [own_value] + right)

    width = 2 * BLOCK + 1
    classes = window(h0_recv, 2, class_f, BLOCK)
    lane = iota((width, 8, LANES), 2)
    row = iota((width, 8, LANES), 1)
    slab = iota((width, 8, LANES), 0) + (me - BLOCK)
    centre = jnp.ones((width, 8, LANES), F32)
    coef = []
    first_last = (
        ((slab == 0) & (row < 4), (slab == n - 1) & (row >= 4)),
        (row % 4 == 0, row % 4 == 3),
        (lane == 0, lane == LANES - 1),
    )
    for direction in range(3):
        speed = pick([vel[k, direction] for k in range(kinds)], classes)
        if kinds == 1:
            speed = jnp.full((width, 8, LANES), speed)
        forward = jnp.maximum(speed, 0.0)
        backward = jnp.minimum(speed, 0.0)
        centre = centre - (forward - backward)
        coef.append(
            (
                jnp.where(first_last[direction][0], 0.0, forward),
                jnp.where(first_last[direction][1], 0.0, -backward),
            )
        )
    kappa = pick([coup[k] for k in range(kinds)], classes)
    answers = []
    for i in range(STEPS):
        answers.append(
            kappa
            * pick([powers[k * STEPS + i : k * STEPS + i + 1, 0:1] for k in range(kinds)], classes)
        )

    upper_half = row >= 4

    def advect(u, keep_from, keep_to):
        span = keep_to - keep_from
        pad = jnp.zeros((1, 8, LANES), F32)
        out = []
        part = slice(keep_from, keep_to)
        for m in range(2):
            x = u[m]
            previous = jnp.concatenate([pad, x[: span - 1]], axis=0)
            following = jnp.concatenate([x[1:], pad], axis=0)
            top = upper_half[part]
            low_x = roll_rows(jnp.where(top, previous, x), 4)
            high_x = roll_rows(jnp.where(top, x, following), 4)
            new = centre[part] * x + coef[0][0][part] * low_x + coef[0][1][part] * high_x
            new = new + coef[1][0][part] * roll_rows(x, 1) + coef[1][1][part] * roll_rows(x, 7)
            new = new + coef[2][0][part] * roll_lanes(x, 1) + coef[2][1][part] * roll_lanes(x, -1)
            out.append(new)
        return out

    def response_of(history, lo, hi, now, part):
        first = jnp.zeros((hi - lo, 8, LANES), F32)
        second = jnp.zeros((hi - lo, 8, LANES), F32)
        for at, (start, v0, v1) in history:
            lag = now - at
            a = v0[lo - start : hi - start]
            b = v1[lo - start : hi - start]
            gain = answers[lag][part]
            first = first + gain * a
            second = second + gain * (b + (MEAN_RATE * lag) * a if lag else b)
        return first, second

    def advect_two(u, lo, hi):
        u = advect(u, lo, hi)
        u = advect(u, lo, hi)
        return [x[1:-1] for x in u]

    def block_steps(u, free):
        history = []
        lo, hi = 0, width
        mine = []
        for s in range(BLOCK):
            u = advect_two(u, lo, hi)
            lo, hi = lo + 1, hi - 1
            part = slice(lo, hi)
            v0 = u[0] + TIME_STEP
            v1 = u[1] + MEAN_RATE * u[0]
            history.append((s, (lo, v0, v1)))
            first, second = response_of(history, lo, hi, s, part)
            gain = kappa[part]
            mine.append((v0[BLOCK - lo], v1[BLOCK - lo]))
            u = [
                v0 + gain * (free[s][0] + first - v0),
                v1 + gain * (free[s][1] + second - v1),
            ]
        return u, mine

    def to_cells(half):
        exchange_arrived(tile_send.at[half], tile_recv.at[half], 1 + half)
        slots = jnp.concatenate([tile_recv[half, s] for s in range(n)], axis=1)
        high, low = two_parts(slots)
        cells = half_dot(jnp.concatenate([high, low], axis=0), hot[...])
        cells = cells[:8] + cells[8:]
        for r in range(8):
            fields[r * 8 : (r + 1) * 8] = cells[:, r * LANES : (r + 1) * LANES]
        return [
            (fields[pl.ds(t, 8, stride=8), :], fields[pl.ds(HALF + t, 8, stride=8), :])
            for t in range(HALF)
        ]

    def to_owners(half, mine):
        for t in range(HALF):
            fields[pl.ds(t, 8, stride=8), :] = mine[t][0]
            fields[pl.ds(HALF + t, 8, stride=8), :] = mine[t][1]
        cells = jnp.concatenate([fields[r * 8 : (r + 1) * 8] for r in range(8)], axis=1)
        high, low = two_parts(cells)
        slots = half_dot(jnp.concatenate([high, low], axis=0), hot[...], NT)
        slots = slots[:8] + slots[8:]
        for e in range(n):
            tile_send[2 + half, e] = slots[:, e * LANES : (e + 1) * LANES]
        exchange_start(tile_send.at[2 + half], tile_recv.at[2 + half], 3 + half)

    early = to_cells(0)
    for t in range(BLOCK - 1):
        h1_send[2 * t] = early[t][0]
        h1_send[2 * t + 1] = early[t][1]
    halo_each(h1_send, h1_recv, 1, BLOCK - 1, lambda d: 2 * (BLOCK - d), "start")
    late = to_cells(1)
    halo_each(h1_send, h1_recv, 1, BLOCK - 1, lambda d: 2 * (BLOCK - d), "arrived")
    moments = [window(h0_recv, m, frac[m], BLOCK) for m in range(2)]
    free = [
        [window(h1_recv, 2 * s + m, early[s][m], BLOCK - 1 - s) for m in range(2)]
        for s in range(BLOCK)
    ]
    moments, mine = block_steps(moments, free)

    own_part = slice(BLOCK, BLOCK + 1)
    h2_send[0] = moments[0][0]
    h2_send[1] = moments[1][0]
    late_free = []
    for t in range(HALF):
        past = [(s, (BLOCK, mine[s][0][None], mine[s][1][None])) for s in range(HALF)]
        first, second = response_of(past, BLOCK, BLOCK + 1, HALF + t, own_part)
        late_free.append((late[t][0] + first[0], late[t][1] + second[0]))
        if t < BLOCK - 1:
            h2_send[2 + 2 * t] = late_free[t][0]
            h2_send[3 + 2 * t] = late_free[t][1]
    halo_each(h2_send, h2_recv, 2, BLOCK, lambda d: 2 + 2 * (BLOCK - d), "start")
    to_owners(0, mine)
    halo_each(h2_send, h2_recv, 2, BLOCK, lambda d: 2 + 2 * (BLOCK - d), "arrived")
    moments = [window(h2_recv, m, moments[m][0], BLOCK) for m in range(2)]
    free = [
        [window(h2_recv, 2 + 2 * s + m, late_free[s][m], BLOCK - 1 - s) for m in range(2)]
        for s in range(BLOCK)
    ]
    moments, mine = block_steps(moments, free)
    to_owners(1, mine)
    age_out[0] = moments[0][0]
    age_out[1] = moments[1][0]

    exchange_arrived(tile_send.at[2], tile_recv.at[2], 3)
    exchange_arrived(tile_send.at[3], tile_recv.at[3], 4)
    first_values = to_columns([tile_recv[2, s] for s in range(n)])
    last_values = to_columns([tile_recv[3, s] for s in range(n)])
    remaining = MEAN_RATE * (STEPS - 1 - row8).astype(F32)
    for c in range(chunks):
        a, b = first_values[c], last_values[c]
        v0 = jnp.where(row8 < HALF, a, roll_rows(b, HALF))
        v1 = jnp.where(row8 < HALF, roll_rows(a, HALF), b)
        v1 = v1 + remaining * v0
        right = []
        for m, value in ((0, v0), (1, v1)):
            pieces = []
            for k in range(kinds):
                belongs = column_class[c] == float(k)
                pieces.append(jnp.where(belongs, coup[k] * value, 0.0))
                pieces.append(jnp.where(belongs & (row8 == m), 1.0, 0.0))
            high, low = two_parts(jnp.concatenate(pieces, axis=0))
            rest = jnp.zeros((LANES - 3 * wide_rows, LANES), BF16)
            right.append(jnp.concatenate([high, low, high, rest], axis=0))
        added = half_dot(response, jnp.concatenate(right, axis=1))
        own0 = main[:, c * LANES : (c + 1) * LANES]
        own1 = main[:, (chunks + c) * LANES : (chunks + c + 1) * LANES]
        mat_out[pl.ds(2 * c, nodes, stride=stride), :] = own0 + added[:, :LANES]
        mat_out[pl.ds(2 * c + 1, nodes, stride=stride), :] = (
            own1 + (STEPS * MEAN_RATE) * own0 + added[:, LANES:]
        )

    exchange_sent(cls_send, cls_recv, 0)
    for which in range(4):
        exchange_sent(tile_send.at[which], tile_recv.at[which], 1 + which)
    halo_each(h0_send, h0_recv, 0, BLOCK, lambda d: 3, "sent")
    halo_each(h1_send, h1_recv, 1, BLOCK - 1, lambda d: 2 * (BLOCK - d), "sent")
    halo_each(h2_send, h2_recv, 2, BLOCK, lambda d: 2 + 2 * (BLOCK - d), "sent")


def shards(fracture, cell_class, owner, matrix, velocity, coupling, operators):
    n = lax.axis_size("gx")
    nodes, _, slots = matrix.shape
    cap = slots // n
    kinds = operators.shape[0]
    chunks = slots // LANES
    flat = matrix.reshape(nodes, 2, chunks, LANES).transpose(0, 2, 1, 3)
    flat = flat.reshape(nodes * chunks * 2, LANES)
    vmem = pl.BlockSpec(memory_space=pltpu.VMEM)
    smem = pl.BlockSpec(memory_space=pltpu.SMEM)
    tall = 2 + 2 * (BLOCK - 1)
    age, out = pl.pallas_call(
        functools.partial(kernel, n, cap, kinds, chunks),
        out_shape=(
            jax.ShapeDtypeStruct((2, 8, LANES), F32),
            jax.ShapeDtypeStruct(flat.shape, F32),
        ),
        in_specs=[vmem, vmem, vmem, pl.BlockSpec(memory_space=pl.ANY), smem, smem, vmem],
        out_specs=(vmem, vmem),
        scratch_shapes=[
            pltpu.VMEM((n * LANES, 8 * LANES), BF16),
            pltpu.VMEM(flat.shape, F32),
            pltpu.VMEM((nodes, 2 * slots), BF16),
            pltpu.VMEM((nodes, 2 * slots), BF16),
            pltpu.VMEM((nodes, 2 * slots), F32),
            pltpu.VMEM((kinds * STEPS, nodes), F32),
            pltpu.VMEM((2 * STEPS, nodes), F32),
            pltpu.VMEM((LANES, nodes), F32),
            pltpu.VMEM((64, LANES), F32),
            pltpu.VMEM((n, 1, LANES), F32),
            pltpu.VMEM((n, 1, LANES), F32),
            pltpu.VMEM((4, n, 8, LANES), F32),
            pltpu.VMEM((4, n, 8, LANES), F32),
            pltpu.VMEM((3, 8, LANES), F32),
            pltpu.VMEM((2, BLOCK, 3, 8, LANES), F32),
            pltpu.VMEM((tall - 2, 8, LANES), F32),
            pltpu.VMEM((2, BLOCK - 1, tall - 2, 8, LANES), F32),
            pltpu.VMEM((tall, 8, LANES), F32),
            pltpu.VMEM((2, BLOCK, tall, 8, LANES), F32),
            pltpu.SemaphoreType.DMA,
            pltpu.SemaphoreType.DMA((5, n)),
            pltpu.SemaphoreType.DMA((5, n)),
            pltpu.SemaphoreType.DMA((3, 2, BLOCK)),
            pltpu.SemaphoreType.DMA((3, 2, BLOCK)),
        ],
        compiler_params=pltpu.CompilerParams(
            collective_id=0, has_side_effects=True, vmem_limit_bytes=48 * 1024 * 1024
        ),
        cost_estimate=pl.CostEstimate(
            flops=2 * 400 * nodes * 2 * slots, bytes_accessed=8 * 2 * nodes * slots, transcendentals=0
        ),
    )(
        fracture.reshape(2, 8, LANES),
        cell_class.reshape(8, LANES),
        owner.reshape(8, LANES),
        flat,
        velocity,
        coupling,
        operators,
    )
    out = out.reshape(nodes, chunks, 2, LANES).transpose(0, 2, 1, 3).reshape(matrix.shape)
    return age.reshape(fracture.shape), out


def solution(mesh):
    in_specs = (
        P(None, ("groups", "gx"), None, None),
        P(("groups", "gx"), None, None),
        P(("groups", "gx"), None, None, None),
        P(None, None, ("groups", "gx")),
        P(),
        P(),
        P(),
    )
    out_specs = (P(None, ("groups", "gx"), None, None), P(None, None, ("groups", "gx")))
    return jax.shard_map(shards, mesh=mesh, in_specs=in_specs, out_specs=out_specs, check_vma=False)
```

```python
import functools

import jax
import jax.numpy as jnp
from jax import lax
from jax.experimental import pallas as pl
from jax.experimental.layout import Layout, with_layout_constraint
from jax.experimental.pallas import tpu as pltpu
from jax.sharding import PartitionSpec as P

STEPS = 8
SUBSTEPS = 2
TIME_STEP = 0.125
MEAN_RATE = 2.0 * TIME_STEP
BLOCK = 4
LANES = 128
HALF = STEPS // 2

F32 = jnp.float32
BF16 = jnp.bfloat16
NN = (((1,), (0,)), ((), ()))
NT = (((1,), (1,)), ((), ()))


def full_dot(a, b, dims=NN):
    return lax.dot_general(a, b, dims, precision=lax.Precision.HIGHEST, preferred_element_type=F32)


def half_dot(a, b, dims=NN):
    return lax.dot_general(a, b, dims, preferred_element_type=F32)


def two_parts(x):
    high = x.astype(BF16)
    low = (x - high.astype(F32)).astype(BF16)
    return high, low


def iota(shape, dim):
    return lax.broadcasted_iota(jnp.int32, shape, dim)


def roll_rows(x, shift):
    return pltpu.roll(x, shift, x.ndim - 2)


def roll_lanes(x, shift):
    shift = shift % LANES
    return x if shift == 0 else pltpu.roll(x, shift, x.ndim - 1)


def kernel(
    n,
    cap,
    kinds,
    chunks,
    frac,
    cls,
    own,
    mat,
    vel,
    coup,
    ops,
    age_out,
    mat_out,
    hot,
    hot_t,
    mat_v,
    s_hi,
    s_lo,
    main,
    rows_pow,
    cols_pow,
    cols_t,
    fields,
    cls_send,
    cls_recv,
    tile_send,
    tile_recv,
    h0_send,
    h0_recv,
    h1_send,
    h1_recv,
    h2_send,
    h2_recv,
    mat_sem,
    a_send_sem,
    a_recv_sem,
    h_send_sem,
    h_recv_sem,
):
    me = lax.axis_index("gx")
    row8 = iota((8, LANES), 0)
    lane8 = iota((8, LANES), 1)

    load = pltpu.make_async_copy(mat, mat_v, mat_sem)
    load.start()

    sides = ((0, -1), (1, 1))
    for d in range(1, BLOCK + 1):
        for side, sign in sides:
            source = me + sign * d

            @pl.when((source < 0) | (source >= n))
            def _():
                h0_recv[side, d - 1] = jnp.zeros(h0_recv.shape[2:], F32)
                h2_recv[side, d - 1] = jnp.zeros(h2_recv.shape[2:], F32)
                if d < BLOCK:
                    h1_recv[side, d - 1] = jnp.zeros(h1_recv.shape[2:], F32)

    barrier = pltpu.get_barrier_semaphore()

    @pl.loop(1, n)
    def _(d):
        pl.semaphore_signal(
            barrier,
            inc=1,
            device_id={"gx": lax.rem(me + d, n)},
            device_id_type=pl.DeviceIdType.MESH,
        )

    def exchange(send, recv, which, d, peer, landing):
        return pltpu.make_async_remote_copy(
            src_ref=send.at[peer],
            dst_ref=recv.at[landing],
            send_sem=a_send_sem.at[which, d],
            recv_sem=a_recv_sem.at[which, landing],
            device_id={"gx": peer},
            device_id_type=pl.DeviceIdType.MESH,
        )

    def exchange_start(send, recv, which):
        @pl.loop(1, n)
        def _(d):
            exchange(send, recv, which, d, lax.rem(me + d, n), me).start()

        recv[me] = send[me]

    def exchange_arrived(send, recv, which):
        @pl.loop(1, n)
        def _(d):
            source = lax.rem(me + n - d, n)
            exchange(send, recv, which, d, source, source).wait_recv()

    def exchange_sent(send, recv, which):
        @pl.loop(1, n)
        def _(d):
            exchange(send, recv, which, d, lax.rem(me + d, n), me).wait_send()

    def halo(send, recv, which, d, side, sign, rows):
        return pltpu.make_async_remote_copy(
            src_ref=send.at[pl.ds(0, rows)],
            dst_ref=recv.at[side, d - 1, pl.ds(0, rows)],
            send_sem=h_send_sem.at[which, side, d - 1],
            recv_sem=h_recv_sem.at[which, side, d - 1],
            device_id={"gx": me - sign * d},
            device_id_type=pl.DeviceIdType.MESH,
        )

    def halo_each(send, recv, which, reach, rows_of, what):
        for d in range(1, reach + 1):
            for side, sign in sides:
                peer = me + sign * d if what == "arrived" else me - sign * d

                @pl.when((peer >= 0) & (peer < n))
                def _():
                    copy = halo(send, recv, which, d, side, sign, rows_of(d))
                    if what == "start":
                        copy.start()
                    elif what == "arrived":
                        copy.wait_recv()
                    else:
                        copy.wait_send()

    owner_f = own[...].astype(F32)
    class_f = cls[...].astype(F32)
    owner_row = iota((n, LANES), 0).astype(F32)
    named = [jnp.where(owner_row == owner_f[r : r + 1, :], 1.0, 0.0) for r in range(8)]
    named_all = jnp.concatenate(named, axis=0).astype(BF16)
    earlier = jnp.where(iota((LANES, LANES), 0) < iota((LANES, LANES), 1), 1.0, 0.0).astype(BF16)
    before = half_dot(named_all, earlier)
    total = half_dot(named_all, jnp.ones((LANES, LANES), BF16))
    base = jnp.zeros((n, LANES), F32)
    places = []
    for r in range(8):
        count = before[r * n : (r + 1) * n] + base
        base = base + total[r * n : (r + 1) * n]
        arrival = jnp.sum(named[r] * count, axis=0, keepdims=True)
        places.append(owner_f[r : r + 1, :] * float(cap) + arrival)
    slot_lane = iota((LANES, LANES), 1).astype(F32)
    for r in range(8):
        place = jnp.broadcast_to(places[r], (LANES, LANES)).T
        for c in range(chunks):
            hit = slot_lane == (place - float(c * LANES))
            hot_t[r * LANES : (r + 1) * LANES, c * LANES : (c + 1) * LANES] = jnp.where(
                hit, 1.0, 0.0
            ).astype(BF16)

    def to_columns(blocks):
        out = [jnp.zeros((8, LANES), F32) for _ in range(chunks)]
        for s in range(n):
            at, off = divmod(s * cap, LANES)
            turned = roll_lanes(blocks[s], off)
            if off + cap <= LANES:
                out[at] = out[at] + turned
            else:
                out[at] = out[at] + jnp.where(lane8 >= off, turned, 0.0)
                out[at + 1] = out[at + 1] + jnp.where(lane8 < off, turned, 0.0)
        return out

    def from_columns(columns):
        out = []
        for s in range(n):
            at, off = divmod(s * cap, LANES)
            block = roll_lanes(columns[at], -off)
            if off + cap > LANES:
                block = jnp.where(lane8 < LANES - off, block, roll_lanes(columns[at + 1], -off))
            out.append(jnp.where(lane8 < cap, block, 0.0))
        return out

    def split_lanes(x):
        return [x[:, c * LANES : (c + 1) * LANES] for c in range(chunks)]

    class_rows = jnp.concatenate(
        [jnp.broadcast_to(class_f[r : r + 1, :], (16, LANES)) for r in range(8)], axis=1
    ).astype(BF16)
    class_out = half_dot(class_rows, hot_t[...])
    for e, block in enumerate(from_columns(split_lanes(class_out[:8]))):
        cls_send[e] = block[0:1]
    h0_send[0] = frac[0]
    h0_send[1] = frac[1]
    h0_send[2] = class_f

    pl.semaphore_wait(barrier, n - 1)
    exchange_start(cls_send, cls_recv, 0)
    halo_each(h0_send, h0_recv, 0, BLOCK, lambda d: 3, "start")

    slot_row = iota((LANES, LANES), 0).astype(F32)
    for c in range(chunks):
        for r in range(8):
            hit = slot_row == (places[r] - float(c * LANES))
            hot[c * LANES : (c + 1) * LANES, r * LANES : (r + 1) * LANES] = jnp.where(
                hit, 1.0, 0.0
            ).astype(BF16)

    rows_pow[...] = jnp.zeros(rows_pow.shape, F32)
    squares, fourths = [], []
    for k in range(kinds):
        first = ops[k]
        square = full_dot(first, first)
        fourth = full_dot(square, square)
        squares.append(square)
        fourths.append(fourth)
        at = k * STEPS
        rows_pow[at : at + 1] = first[0:1]
        rows_pow[at + 1 : at + 2] = square[0:1]
        rows_pow[at + 2 : at + 4] = full_dot(rows_pow[at : at + 8], square)[0:2]
        rows_pow[at + 4 : at + 8] = full_dot(rows_pow[at : at + 8], fourth)[0:4]

    load.wait()
    stride = 2 * chunks
    for m in range(2):
        for c in range(chunks):
            at = (m * chunks + c) * LANES
            block = mat_v[pl.ds(c * 2 + m, LANES, stride=stride), :]
            high, low = two_parts(block)
            s_hi[:, at : at + LANES] = high
            s_lo[:, at : at + LANES] = low

    powers = rows_pow[...]
    p_high, p_low = two_parts(powers)
    wide = half_dot(jnp.concatenate([p_high, p_low], axis=0), s_hi[...])
    count = kinds * STEPS
    q_all = wide[:count] + wide[count:] + half_dot(p_high, s_lo[...])

    exchange_arrived(cls_send, cls_recv, 0)

    column_class = to_columns([jnp.broadcast_to(cls_recv[s], (8, LANES)) for s in range(n)])

    steady0, steady1 = [], []
    for k in range(kinds):
        sums = jnp.sum(powers[k * STEPS : (k + 1) * STEPS], axis=1, keepdims=True)
        sums = jnp.broadcast_to(sums, (STEPS, LANES))
        zero_sum = jnp.zeros((STEPS, LANES), F32)
        one_sum = jnp.zeros((STEPS, LANES), F32)
        for i in range(STEPS):
            term = jnp.where(row8 >= i, sums[i : i + 1], 0.0)
            zero_sum = zero_sum + TIME_STEP * term
            one_sum = one_sum + (TIME_STEP * MEAN_RATE * i) * term
        steady0.append(zero_sum)
        steady1.append(one_sum)

    def pick(options, which):
        value = options[0]
        for k in range(1, kinds):
            value = jnp.where(which == float(k), options[k], value)
        return value

    step_row = (row8 + 1).astype(F32)
    tiles_a, tiles_b = [], []
    for c in range(chunks):
        parts = []
        for m in range(2):
            at = (m * chunks + c) * LANES
            parts.append(
                pick(
                    [q_all[k * STEPS : (k + 1) * STEPS, at : at + LANES] for k in range(kinds)],
                    column_class[c],
                )
            )
        free0 = parts[0] + pick(steady0, column_class[c])
        free1 = parts[1] + MEAN_RATE * step_row * parts[0] + pick(steady1, column_class[c])
        tiles_a.append(jnp.where(row8 < HALF, free0, roll_rows(free1, HALF)))
        tiles_b.append(jnp.where(row8 < HALF, roll_rows(free0, HALF), free1))
    for half, tiles in ((0, tiles_a), (1, tiles_b)):
        blocks = from_columns(tiles)
        for e in range(n):
            tile_send[half, e] = blocks[e]
        exchange_start(tile_send.at[half], tile_recv.at[half], 1 + half)

    eights = [full_dot(fourths[k], fourths[k]) for k in range(kinds)]
    e_high, e_low = two_parts(jnp.concatenate(eights, axis=0))
    nodes = eights[0].shape[0]
    for b in range(chunks):
        lanes = slice(b * 2 * LANES, (b + 1) * 2 * LANES)
        right = s_hi[:, lanes]
        both = half_dot(e_high, right) + half_dot(e_low, right) + half_dot(e_high, s_lo[:, lanes])
        for i in range(2):
            at = b * 2 + i
            which = column_class[at % chunks][0:1]
            main[:, at * LANES : (at + 1) * LANES] = pick(
                [
                    both[k * nodes : (k + 1) * nodes, i * LANES : (i + 1) * LANES]
                    for k in range(kinds)
                ],
                which,
            )

    wide_rows = kinds * 16
    cols_t[...] = jnp.zeros(cols_t.shape, F32)
    for k in range(kinds):
        turned = ops[k].T
        cols_pow[...] = jnp.zeros(cols_pow.shape, F32)
        cols_pow[0:1] = turned[0:1]
        cols_pow[1:2] = jnp.sum(turned, axis=0, keepdims=True)
        cols_pow[2:4] = full_dot(cols_pow[0:8], ops[k], NT)[0:2]
        cols_pow[4:8] = full_dot(cols_pow[0:8], squares[k], NT)[0:4]
        cols_pow[8:16] = full_dot(cols_pow[0:8], fourths[k], NT)
        zero_sum = jnp.zeros((1, LANES), F32)
        one_sum = jnp.zeros((1, LANES), F32)
        for i in range(STEPS):
            cols_t[k * 16 + 7 - i : k * 16 + 8 - i] = cols_pow[2 * i : 2 * i + 1]
            source_row = cols_pow[2 * i + 1 : 2 * i + 2]
            zero_sum = zero_sum + TIME_STEP * source_row
            one_sum = one_sum + (TIME_STEP * MEAN_RATE * i) * source_row
        cols_t[k * 16 + 8 : k * 16 + 9] = zero_sum
        cols_t[k * 16 + 9 : k * 16 + 10] = one_sum
    whole = cols_t[0:wide_rows]
    whole_high = whole.astype(BF16).astype(F32)
    cols_t[0:wide_rows] = whole_high
    cols_t[wide_rows : 2 * wide_rows] = whole_high
    cols_t[2 * wide_rows : 3 * wide_rows] = whole - whole_high
    response = cols_t[...].T.astype(BF16)

    halo_each(h0_send, h0_recv, 0, BLOCK, lambda d: 3, "arrived")

    def window(recv, index, own_value, reach):
        left = [recv[0, d - 1, index] for d in range(reach, 0, -1)]
        right = [recv[1, d - 1, index] for d in range(1, reach + 1)]
        return jnp.stack(left + [own_value] + right)

    width = 2 * BLOCK + 1
    classes = window(h0_recv, 2, class_f, BLOCK)
    lane = iota((width, 8, LANES), 2)
    row = iota((width, 8, LANES), 1)
    slab = iota((width, 8, LANES), 0) + (me - BLOCK)
    centre = jnp.ones((width, 8, LANES), F32)
    coef = []
    first_last = (
        ((slab == 0) & (row < 4), (slab == n - 1) & (row >= 4)),
        (row % 4 == 0, row % 4 == 3),
        (lane == 0, lane == LANES - 1),
    )
    for direction in range(3):
        speed = pick([vel[k, direction] for k in range(kinds)], classes)
        if kinds == 1:
            speed = jnp.full((width, 8, LANES), speed)
        forward = jnp.maximum(speed, 0.0)
        backward = jnp.minimum(speed, 0.0)
        centre = centre - (forward - backward)
        coef.append(
            (
                jnp.where(first_last[direction][0], 0.0, forward),
                jnp.where(first_last[direction][1], 0.0, -backward),
            )
        )
    kappa = pick([coup[k] for k in range(kinds)], classes)
    answers = []
    for i in range(STEPS):
        answers.append(
            kappa
            * pick([powers[k * STEPS + i : k * STEPS + i + 1, 0:1] for k in range(kinds)], classes)
        )

    upper_half = row >= 4

    def advect(u, keep_from, keep_to):
        span = keep_to - keep_from
        pad = jnp.zeros((1, 8, LANES), F32)
        out = []
        part = slice(keep_from, keep_to)
        for m in range(2):
            x = u[m]
            previous = jnp.concatenate([pad, x[: span - 1]], axis=0)
            following = jnp.concatenate([x[1:], pad], axis=0)
            top = upper_half[part]
            low_x = roll_rows(jnp.where(top, previous, x), 4)
            high_x = roll_rows(jnp.where(top, x, following), 4)
            new = centre[part] * x + coef[0][0][part] * low_x + coef[0][1][part] * high_x
            new = new + coef[1][0][part] * roll_rows(x, 1) + coef[1][1][part] * roll_rows(x, 7)
            new = new + coef[2][0][part] * roll_lanes(x, 1) + coef[2][1][part] * roll_lanes(x, -1)
            out.append(new)
        return out

    def response_of(history, lo, hi, now, part):
        first = jnp.zeros((hi - lo, 8, LANES), F32)
        second = jnp.zeros((hi - lo, 8, LANES), F32)
        for at, (start, v0, v1) in history:
            lag = now - at
            a = v0[lo - start : hi - start]
            b = v1[lo - start : hi - start]
            gain = answers[lag][part]
            first = first + gain * a
            second = second + gain * (b + (MEAN_RATE * lag) * a if lag else b)
        return first, second

    def advect_two(u, lo, hi):
        u = advect(u, lo, hi)
        u = advect(u, lo, hi)
        return [x[1:-1] for x in u]

    def block_steps(u, free):
        history = []
        lo, hi = 0, width
        mine = []
        for s in range(BLOCK):
            u = advect_two(u, lo, hi)
            lo, hi = lo + 1, hi - 1
            part = slice(lo, hi)
            v0 = u[0] + TIME_STEP
            v1 = u[1] + MEAN_RATE * u[0]
            history.append((s, (lo, v0, v1)))
            first, second = response_of(history, lo, hi, s, part)
            gain = kappa[part]
            mine.append((v0[BLOCK - lo], v1[BLOCK - lo]))
            u = [
                v0 + gain * (free[s][0] + first - v0),
                v1 + gain * (free[s][1] + second - v1),
            ]
        return u, mine

    def to_cells(half):
        exchange_arrived(tile_send.at[half], tile_recv.at[half], 1 + half)
        slots = jnp.concatenate(to_columns([tile_recv[half, s] for s in range(n)]), axis=1)
        high, low = two_parts(slots)
        cells = half_dot(jnp.concatenate([high, low], axis=0), hot[...])
        cells = cells[:8] + cells[8:]
        for r in range(8):
            fields[r * 8 : (r + 1) * 8] = cells[:, r * LANES : (r + 1) * LANES]
        return [
            (fields[pl.ds(t, 8, stride=8), :], fields[pl.ds(HALF + t, 8, stride=8), :])
            for t in range(HALF)
        ]

    def to_owners(half, mine):
        for t in range(HALF):
            fields[pl.ds(t, 8, stride=8), :] = mine[t][0]
            fields[pl.ds(HALF + t, 8, stride=8), :] = mine[t][1]
        cells = jnp.concatenate([fields[r * 8 : (r + 1) * 8] for r in range(8)], axis=1)
        high, low = two_parts(cells)
        slots = half_dot(jnp.concatenate([high, low], axis=0), hot_t[...])
        for e, block in enumerate(from_columns(split_lanes(slots[:8] + slots[8:]))):
            tile_send[2 + half, e] = block
        exchange_start(tile_send.at[2 + half], tile_recv.at[2 + half], 3 + half)

    early = to_cells(0)
    for t in range(BLOCK - 1):
        h1_send[2 * t] = early[t][0]
        h1_send[2 * t + 1] = early[t][1]
    halo_each(h1_send, h1_recv, 1, BLOCK - 1, lambda d: 2 * (BLOCK - d), "start")
    late = to_cells(1)
    halo_each(h1_send, h1_recv, 1, BLOCK - 1, lambda d: 2 * (BLOCK - d), "arrived")
    moments = [window(h0_recv, m, frac[m], BLOCK) for m in range(2)]
    free = [
        [window(h1_recv, 2 * s + m, early[s][m], BLOCK - 1 - s) for m in range(2)]
        for s in range(BLOCK)
    ]
    moments, mine = block_steps(moments, free)

    own_part = slice(BLOCK, BLOCK + 1)
    h2_send[0] = moments[0][0]
    h2_send[1] = moments[1][0]
    late_free = []
    for t in range(HALF):
        past = [(s, (BLOCK, mine[s][0][None], mine[s][1][None])) for s in range(HALF)]
        first, second = response_of(past, BLOCK, BLOCK + 1, HALF + t, own_part)
        late_free.append((late[t][0] + first[0], late[t][1] + second[0]))
        if t < BLOCK - 1:
            h2_send[2 + 2 * t] = late_free[t][0]
            h2_send[3 + 2 * t] = late_free[t][1]
    halo_each(h2_send, h2_recv, 2, BLOCK, lambda d: 2 + 2 * (BLOCK - d), "start")
    to_owners(0, mine)
    halo_each(h2_send, h2_recv, 2, BLOCK, lambda d: 2 + 2 * (BLOCK - d), "arrived")
    moments = [window(h2_recv, m, moments[m][0], BLOCK) for m in range(2)]
    free = [
        [window(h2_recv, 2 + 2 * s + m, late_free[s][m], BLOCK - 1 - s) for m in range(2)]
        for s in range(BLOCK)
    ]
    moments, mine = block_steps(moments, free)
    to_owners(1, mine)
    age_out[0] = moments[0][0]
    age_out[1] = moments[1][0]

    exchange_arrived(tile_send.at[2], tile_recv.at[2], 3)
    exchange_arrived(tile_send.at[3], tile_recv.at[3], 4)
    first_values = to_columns([tile_recv[2, s] for s in range(n)])
    last_values = to_columns([tile_recv[3, s] for s in range(n)])
    remaining = MEAN_RATE * (STEPS - 1 - row8).astype(F32)
    for c in range(chunks):
        a, b = first_values[c], last_values[c]
        v0 = jnp.where(row8 < HALF, a, roll_rows(b, HALF))
        v1 = jnp.where(row8 < HALF, roll_rows(a, HALF), b)
        v1 = v1 + remaining * v0
        right = []
        for m, value in ((0, v0), (1, v1)):
            pieces = []
            for k in range(kinds):
                belongs = column_class[c] == float(k)
                pieces.append(jnp.where(belongs, coup[k] * value, 0.0))
                pieces.append(jnp.where(belongs & (row8 == m), 1.0, 0.0))
            high, low = two_parts(jnp.concatenate(pieces, axis=0))
            rest = jnp.zeros((LANES - 3 * wide_rows, LANES), BF16)
            right.append(jnp.concatenate([high, low, high, rest], axis=0))
        added = half_dot(response, jnp.concatenate(right, axis=1))
        own0 = main[:, c * LANES : (c + 1) * LANES]
        own1 = main[:, (chunks + c) * LANES : (chunks + c + 1) * LANES]
        mat_out[pl.ds(2 * c, nodes, stride=stride), :] = own0 + added[:, :LANES]
        mat_out[pl.ds(2 * c + 1, nodes, stride=stride), :] = (
            own1 + (STEPS * MEAN_RATE) * own0 + added[:, LANES:]
        )

    exchange_sent(cls_send, cls_recv, 0)
    for which in range(4):
        exchange_sent(tile_send.at[which], tile_recv.at[which], 1 + which)
    halo_each(h0_send, h0_recv, 0, BLOCK, lambda d: 3, "sent")
    halo_each(h1_send, h1_recv, 1, BLOCK - 1, lambda d: 2 * (BLOCK - d), "sent")
    halo_each(h2_send, h2_recv, 2, BLOCK, lambda d: 2 + 2 * (BLOCK - d), "sent")


def shards(fracture, cell_class, owner, matrix, velocity, coupling, operators):
    n = lax.axis_size("gx")
    nodes, _, slots = matrix.shape
    cap = slots // n
    kinds = operators.shape[0]
    chunks = slots // LANES
    tiled = Layout((0, 2, 1, 3))
    flat = with_layout_constraint(matrix.reshape(nodes, 2, chunks, LANES), tiled)
    flat = flat.transpose(0, 2, 1, 3)
    flat = flat.reshape(nodes * chunks * 2, LANES)
    vmem = pl.BlockSpec(memory_space=pltpu.VMEM)
    smem = pl.BlockSpec(memory_space=pltpu.SMEM)
    tall = 2 + 2 * (BLOCK - 1)
    age, out = pl.pallas_call(
        functools.partial(kernel, n, cap, kinds, chunks),
        out_shape=(
            jax.ShapeDtypeStruct((2, 8, LANES), F32),
            jax.ShapeDtypeStruct(flat.shape, F32),
        ),
        in_specs=[vmem, vmem, vmem, pl.BlockSpec(memory_space=pl.ANY), smem, smem, vmem],
        out_specs=(vmem, vmem),
        scratch_shapes=[
            pltpu.VMEM((slots, 8 * LANES), BF16),
            pltpu.VMEM((8 * LANES, slots), BF16),
            pltpu.VMEM(flat.shape, F32),
            pltpu.VMEM((nodes, 2 * slots), BF16),
            pltpu.VMEM((nodes, 2 * slots), BF16),
            pltpu.VMEM((nodes, 2 * slots), F32),
            pltpu.VMEM((kinds * STEPS, nodes), F32),
            pltpu.VMEM((2 * STEPS, nodes), F32),
            pltpu.VMEM((LANES, nodes), F32),
            pltpu.VMEM((64, LANES), F32),
            pltpu.VMEM((n, 1, LANES), F32),
            pltpu.VMEM((n, 1, LANES), F32),
            pltpu.VMEM((4, n, 8, LANES), F32),
            pltpu.VMEM((4, n, 8, LANES), F32),
            pltpu.VMEM((3, 8, LANES), F32),
            pltpu.VMEM((2, BLOCK, 3, 8, LANES), F32),
            pltpu.VMEM((tall - 2, 8, LANES), F32),
            pltpu.VMEM((2, BLOCK - 1, tall - 2, 8, LANES), F32),
            pltpu.VMEM((tall, 8, LANES), F32),
            pltpu.VMEM((2, BLOCK, tall, 8, LANES), F32),
            pltpu.SemaphoreType.DMA,
            pltpu.SemaphoreType.DMA((5, n)),
            pltpu.SemaphoreType.DMA((5, n)),
            pltpu.SemaphoreType.DMA((3, 2, BLOCK)),
            pltpu.SemaphoreType.DMA((3, 2, BLOCK)),
        ],
        compiler_params=pltpu.CompilerParams(
            collective_id=0, has_side_effects=True, vmem_limit_bytes=48 * 1024 * 1024
        ),
        cost_estimate=pl.CostEstimate(
            flops=2 * 400 * nodes * 2 * slots, bytes_accessed=8 * 2 * nodes * slots, transcendentals=0
        ),
    )(
        fracture.reshape(2, 8, LANES),
        cell_class.reshape(8, LANES),
        owner.reshape(8, LANES),
        flat,
        velocity,
        coupling,
        operators,
    )
    out = out.reshape(nodes, chunks, 2, LANES).transpose(0, 2, 1, 3)
    out = with_layout_constraint(out, tiled).reshape(matrix.shape)
    return age.reshape(fracture.shape), out


def solution(mesh):
    in_specs = (
        P(None, ("groups", "gx"), None, None),
        P(("groups", "gx"), None, None),
        P(("groups", "gx"), None, None, None),
        P(None, None, ("groups", "gx")),
        P(),
        P(),
        P(),
    )
    out_specs = (P(None, ("groups", "gx"), None, None), P(None, None, ("groups", "gx")))
    return jax.shard_map(shards, mesh=mesh, in_specs=in_specs, out_specs=out_specs, check_vma=False)
```

```python
import functools

import jax
import jax.numpy as jnp
from jax import lax
from jax.experimental import pallas as pl
from jax.experimental.layout import Layout, with_layout_constraint
from jax.experimental.pallas import tpu as pltpu
from jax.sharding import PartitionSpec as P

STEPS = 8
SUBSTEPS = 2
TIME_STEP = 0.125
MEAN_RATE = 2.0 * TIME_STEP
BLOCK = 4
LANES = 128
VMEM_BYTES = 63 * 1024 * 1024
HALF = STEPS // 2

F32 = jnp.float32
BF16 = jnp.bfloat16
NN = (((1,), (0,)), ((), ()))
NT = (((1,), (1,)), ((), ()))


def full_dot(a, b, dims=NN):
    return lax.dot_general(a, b, dims, precision=lax.Precision.HIGHEST, preferred_element_type=F32)


def half_dot(a, b, dims=NN):
    return lax.dot_general(a, b, dims, preferred_element_type=F32)


def two_parts(x):
    high = x.astype(BF16)
    low = (x - high.astype(F32)).astype(BF16)
    return high, low


def iota(shape, dim):
    return lax.broadcasted_iota(jnp.int32, shape, dim)


def roll_rows(x, shift):
    return pltpu.roll(x, shift, x.ndim - 2)


def roll_lanes(x, shift):
    shift = shift % LANES
    return x if shift == 0 else pltpu.roll(x, shift, x.ndim - 1)


def pick(options, which):
    value = options[0]
    for k in range(1, len(options)):
        value = jnp.where(which == float(k), options[k], value)
    return value


def finish(
    kinds,
    chunks,
    age_any,
    main_any,
    pack_any,
    response_any,
    coup_any,
    age_out,
    mat_out,
    age_v,
    main_v,
    pack,
    response_v,
    coup,
    added,
    load_sem,
    store_sem,
):
    nodes = response_any.shape[0]
    stride = 2 * chunks
    bands = 4
    band = nodes // bands
    rows = band * stride

    def band_rows(i):
        return pl.ds(i * rows, rows)

    pairs = [(pack_any, pack), (response_any, response_v), (coup_any, coup), (age_any, age_v)]
    pairs += [(main_any.at[band_rows(i)], main_v.at[band_rows(i)]) for i in range(bands)]
    loads = [
        pltpu.make_async_copy(source, target, load_sem.at[i])
        for i, (source, target) in enumerate(pairs)
    ]
    for load in loads:
        load.start()
    for load in loads[:4]:
        load.wait()
    age_store = pltpu.make_async_copy(age_v, age_out, store_sem.at[bands])
    age_store.start()
    row8 = iota((8, LANES), 0)
    wide_rows = kinds * 16
    remaining = MEAN_RATE * (STEPS - 1 - row8).astype(F32)
    rest = jnp.zeros((LANES - 3 * wide_rows, LANES), BF16)
    right = []
    for c in range(chunks):
        a, b, which = pack[0, c], pack[1, c], pack[2, c]
        v0 = jnp.where(row8 < HALF, a, roll_rows(b, HALF))
        v1 = jnp.where(row8 < HALF, roll_rows(a, HALF), b)
        v1 = v1 + remaining * v0
        for m, value in ((0, v0), (1, v1)):
            pieces = []
            for k in range(kinds):
                belongs = which == float(k)
                pieces.append(jnp.where(belongs, coup[:, k : k + 1] * value, 0.0))
                pieces.append(jnp.where(belongs & (row8 == m), 1.0, 0.0))
            high, low = two_parts(jnp.concatenate(pieces, axis=0))
            right.append(jnp.concatenate([high, low, high, rest], axis=0))
    added[...] = half_dot(response_v[...].astype(BF16), jnp.concatenate(right, axis=1))
    stores = []
    for i in range(bands):
        loads[4 + i].wait()
        for at in range(stride):
            where = pl.ds(i * rows + at, band, stride=stride)
            more = added[i * band : (i + 1) * band, at * LANES : (at + 1) * LANES]
            main_v[where, :] = main_v[where, :] + more
        store = pltpu.make_async_copy(
            main_v.at[band_rows(i)], mat_out.at[band_rows(i)], store_sem.at[i]
        )
        store.start()
        stores.append(store)
    for store in stores:
        store.wait()
    age_store.wait()


def kernel(
    n,
    cap,
    kinds,
    chunks,
    frac_any,
    cls_any,
    own_any,
    mat,
    vel_any,
    coup_any,
    ops_any,
    age_out,
    main_any,
    pack_out,
    response_out,
    hot,
    hot_t,
    mat_v,
    s_hi,
    s_lo,
    main,
    rows_pow,
    cols_pow,
    cols_t,
    fields,
    cls_send,
    cls_recv,
    tile_send,
    tile_recv,
    h0_send,
    h0_recv,
    h1_send,
    h1_recv,
    h2_send,
    h2_recv,
    frac,
    cls,
    own,
    vel,
    coup,
    ops,
    load_sem,
    store_sem,
    a_send_sem,
    a_recv_sem,
    h_send_sem,
    h_recv_sem,
):
    me = lax.axis_index("gx")
    row8 = iota((8, LANES), 0)
    lane8 = iota((8, LANES), 1)

    loads = [
        pltpu.make_async_copy(source, target, load_sem.at[i])
        for i, (source, target) in enumerate(
            (
                (own_any, own),
                (cls_any, cls),
                (frac_any, frac),
                (ops_any, ops),
                (mat, mat_v),
                (vel_any, vel),
                (coup_any, coup),
            )
        )
    ]
    for load in loads:
        load.start()

    sides = ((0, -1), (1, 1))
    for d in range(1, BLOCK + 1):
        for side, sign in sides:
            source = me + sign * d

            @pl.when((source < 0) | (source >= n))
            def _():
                h0_recv[side, d - 1] = jnp.zeros(h0_recv.shape[2:], F32)
                h2_recv[side, d - 1] = jnp.zeros(h2_recv.shape[2:], F32)
                if d < BLOCK:
                    h1_recv[side, d - 1] = jnp.zeros(h1_recv.shape[2:], F32)

    barrier = pltpu.get_barrier_semaphore()

    @pl.loop(1, n)
    def _(d):
        pl.semaphore_signal(
            barrier,
            inc=1,
            device_id={"gx": lax.rem(me + d, n)},
            device_id_type=pl.DeviceIdType.MESH,
        )

    def exchange(send, recv, which, d, peer, landing):
        return pltpu.make_async_remote_copy(
            src_ref=send.at[peer],
            dst_ref=recv.at[landing],
            send_sem=a_send_sem.at[which, d],
            recv_sem=a_recv_sem.at[which, landing],
            device_id={"gx": peer},
            device_id_type=pl.DeviceIdType.MESH,
        )

    def exchange_start(send, recv, which):
        @pl.loop(1, n)
        def _(d):
            exchange(send, recv, which, d, lax.rem(me + d, n), me).start()

        recv[me] = send[me]

    def exchange_arrived(send, recv, which):
        @pl.loop(1, n)
        def _(d):
            source = lax.rem(me + n - d, n)
            exchange(send, recv, which, d, source, source).wait_recv()

    def exchange_sent(send, recv, which):
        @pl.loop(1, n)
        def _(d):
            exchange(send, recv, which, d, lax.rem(me + d, n), me).wait_send()

    def halo(send, recv, which, d, side, sign, rows):
        return pltpu.make_async_remote_copy(
            src_ref=send.at[pl.ds(0, rows)],
            dst_ref=recv.at[side, d - 1, pl.ds(0, rows)],
            send_sem=h_send_sem.at[which, side, d - 1],
            recv_sem=h_recv_sem.at[which, side, d - 1],
            device_id={"gx": me - sign * d},
            device_id_type=pl.DeviceIdType.MESH,
        )

    def halo_each(send, recv, which, reach, rows_of, what):
        for d in range(1, reach + 1):
            for side, sign in sides:
                peer = me + sign * d if what == "arrived" else me - sign * d

                @pl.when((peer >= 0) & (peer < n))
                def _():
                    copy = halo(send, recv, which, d, side, sign, rows_of(d))
                    if what == "start":
                        copy.start()
                    elif what == "arrived":
                        copy.wait_recv()
                    else:
                        copy.wait_send()

    loads[0].wait()
    loads[1].wait()
    owner_f = own[...].astype(F32)
    class_f = cls[...].astype(F32)
    owner_row = iota((n, LANES), 0).astype(F32)
    named = [jnp.where(owner_row == owner_f[r : r + 1, :], 1.0, 0.0) for r in range(8)]
    named_all = jnp.concatenate(named, axis=0).astype(BF16)
    earlier = jnp.where(iota((LANES, LANES), 0) < iota((LANES, LANES), 1), 1.0, 0.0).astype(BF16)
    before = half_dot(named_all, earlier)
    total = half_dot(named_all, jnp.ones((LANES, LANES), BF16))
    base = jnp.zeros((n, LANES), F32)
    places = []
    for r in range(8):
        count = before[r * n : (r + 1) * n] + base
        base = base + total[r * n : (r + 1) * n]
        arrival = jnp.sum(named[r] * count, axis=0, keepdims=True)
        places.append(owner_f[r : r + 1, :] * float(cap) + arrival)
    slot_lane = iota((LANES, LANES), 1).astype(F32)
    for r in range(8):
        place = jnp.broadcast_to(places[r], (LANES, LANES)).T
        for c in range(chunks):
            hit = slot_lane == (place - float(c * LANES))
            hot_t[r * LANES : (r + 1) * LANES, c * LANES : (c + 1) * LANES] = jnp.where(
                hit, 1.0, 0.0
            ).astype(BF16)

    def to_columns(blocks):
        out = [jnp.zeros((8, LANES), F32) for _ in range(chunks)]
        for s in range(n):
            at, off = divmod(s * cap, LANES)
            turned = roll_lanes(blocks[s], off)
            if off + cap <= LANES:
                out[at] = out[at] + turned
            else:
                out[at] = out[at] + jnp.where(lane8 >= off, turned, 0.0)
                out[at + 1] = out[at + 1] + jnp.where(lane8 < off, turned, 0.0)
        return out

    def from_columns(columns):
        out = []
        for s in range(n):
            at, off = divmod(s * cap, LANES)
            block = roll_lanes(columns[at], -off)
            if off + cap > LANES:
                block = jnp.where(lane8 < LANES - off, block, roll_lanes(columns[at + 1], -off))
            out.append(jnp.where(lane8 < cap, block, 0.0))
        return out

    def split_lanes(x):
        return [x[:, c * LANES : (c + 1) * LANES] for c in range(chunks)]

    class_rows = jnp.concatenate(
        [jnp.broadcast_to(class_f[r : r + 1, :], (16, LANES)) for r in range(8)], axis=1
    ).astype(BF16)
    class_out = half_dot(class_rows, hot_t[...])
    for e, block in enumerate(from_columns(split_lanes(class_out[:8]))):
        cls_send[e] = block[0:1]
    loads[2].wait()
    h0_send[0] = frac[0]
    h0_send[1] = frac[1]
    h0_send[2] = class_f

    pl.semaphore_wait(barrier, n - 1)
    exchange_start(cls_send, cls_recv, 0)
    halo_each(h0_send, h0_recv, 0, BLOCK, lambda d: 3, "start")

    slot_row = iota((LANES, LANES), 0).astype(F32)
    for c in range(chunks):
        for r in range(8):
            hit = slot_row == (places[r] - float(c * LANES))
            hot[c * LANES : (c + 1) * LANES, r * LANES : (r + 1) * LANES] = jnp.where(
                hit, 1.0, 0.0
            ).astype(BF16)

    loads[3].wait()
    rows_pow[...] = jnp.zeros(rows_pow.shape, F32)
    squares, fourths = [], []
    for k in range(kinds):
        first = ops[k]
        square = full_dot(first, first)
        fourth = full_dot(square, square)
        squares.append(square)
        fourths.append(fourth)
        at = k * STEPS
        rows_pow[at : at + 1] = first[0:1]
        rows_pow[at + 1 : at + 2] = square[0:1]
        rows_pow[at + 2 : at + 4] = full_dot(rows_pow[at : at + 8], square)[0:2]
        rows_pow[at + 4 : at + 8] = full_dot(rows_pow[at : at + 8], fourth)[0:4]

    for load in loads[4:]:
        load.wait()
    stride = 2 * chunks
    for m in range(2):
        for c in range(chunks):
            at = (m * chunks + c) * LANES
            block = mat_v[pl.ds(c * 2 + m, LANES, stride=stride), :]
            high, low = two_parts(block)
            s_hi[:, at : at + LANES] = high
            s_lo[:, at : at + LANES] = low

    powers = rows_pow[...]
    p_high, p_low = two_parts(powers)
    wide = half_dot(jnp.concatenate([p_high, p_low], axis=0), s_hi[...])
    count = kinds * STEPS
    q_all = wide[:count] + wide[count:] + half_dot(p_high, s_lo[...])

    exchange_arrived(cls_send, cls_recv, 0)

    column_class = to_columns([jnp.broadcast_to(cls_recv[s], (8, LANES)) for s in range(n)])

    steady0, steady1 = [], []
    for k in range(kinds):
        sums = jnp.sum(powers[k * STEPS : (k + 1) * STEPS], axis=1, keepdims=True)
        sums = jnp.broadcast_to(sums, (STEPS, LANES))
        zero_sum = jnp.zeros((STEPS, LANES), F32)
        one_sum = jnp.zeros((STEPS, LANES), F32)
        for i in range(STEPS):
            term = jnp.where(row8 >= i, sums[i : i + 1], 0.0)
            zero_sum = zero_sum + TIME_STEP * term
            one_sum = one_sum + (TIME_STEP * MEAN_RATE * i) * term
        steady0.append(zero_sum)
        steady1.append(one_sum)

    step_row = (row8 + 1).astype(F32)
    tiles_a, tiles_b = [], []
    for c in range(chunks):
        parts = []
        for m in range(2):
            at = (m * chunks + c) * LANES
            parts.append(
                pick(
                    [q_all[k * STEPS : (k + 1) * STEPS, at : at + LANES] for k in range(kinds)],
                    column_class[c],
                )
            )
        free0 = parts[0] + pick(steady0, column_class[c])
        free1 = parts[1] + MEAN_RATE * step_row * parts[0] + pick(steady1, column_class[c])
        tiles_a.append(jnp.where(row8 < HALF, free0, roll_rows(free1, HALF)))
        tiles_b.append(jnp.where(row8 < HALF, roll_rows(free0, HALF), free1))
    for half, tiles in ((0, tiles_a), (1, tiles_b)):
        blocks = from_columns(tiles)
        for e in range(n):
            tile_send[half, e] = blocks[e]
        exchange_start(tile_send.at[half], tile_recv.at[half], 1 + half)

    eights = [full_dot(fourths[k], fourths[k]) for k in range(kinds)]
    e_high, e_low = two_parts(jnp.concatenate(eights, axis=0))
    nodes = eights[0].shape[0]
    for b in range(chunks):
        lanes = slice(b * 2 * LANES, (b + 1) * 2 * LANES)
        right = s_hi[:, lanes]
        both = half_dot(e_high, right) + half_dot(e_low, right) + half_dot(e_high, s_lo[:, lanes])
        for i in range(2):
            at = b * 2 + i
            m, c = divmod(at, chunks)
            value = pick(
                [
                    both[k * nodes : (k + 1) * nodes, i * LANES : (i + 1) * LANES]
                    for k in range(kinds)
                ],
                column_class[c][0:1],
            )
            if m == 1:
                mean = main[pl.ds(2 * c, nodes, stride=stride), :]
                value = value + (STEPS * MEAN_RATE) * mean
            main[pl.ds(2 * c + m, nodes, stride=stride), :] = value
    store = pltpu.make_async_copy(main, main_any, store_sem)
    store.start()

    wide_rows = kinds * 16
    cols_t[...] = jnp.zeros(cols_t.shape, F32)
    for k in range(kinds):
        turned = ops[k].T
        cols_pow[...] = jnp.zeros(cols_pow.shape, F32)
        cols_pow[0:1] = turned[0:1]
        cols_pow[1:2] = jnp.sum(turned, axis=0, keepdims=True)
        cols_pow[2:4] = full_dot(cols_pow[0:8], ops[k], NT)[0:2]
        cols_pow[4:8] = full_dot(cols_pow[0:8], squares[k], NT)[0:4]
        cols_pow[8:16] = full_dot(cols_pow[0:8], fourths[k], NT)
        zero_sum = jnp.zeros((1, LANES), F32)
        one_sum = jnp.zeros((1, LANES), F32)
        for i in range(STEPS):
            cols_t[k * 16 + 7 - i : k * 16 + 8 - i] = cols_pow[2 * i : 2 * i + 1]
            source_row = cols_pow[2 * i + 1 : 2 * i + 2]
            zero_sum = zero_sum + TIME_STEP * source_row
            one_sum = one_sum + (TIME_STEP * MEAN_RATE * i) * source_row
        cols_t[k * 16 + 8 : k * 16 + 9] = zero_sum
        cols_t[k * 16 + 9 : k * 16 + 10] = one_sum
    whole = cols_t[0:wide_rows]
    whole_high = whole.astype(BF16).astype(F32)
    cols_t[0:wide_rows] = whole_high
    cols_t[wide_rows : 2 * wide_rows] = whole_high
    cols_t[2 * wide_rows : 3 * wide_rows] = whole - whole_high
    response_out[...] = cols_t[...].T

    halo_each(h0_send, h0_recv, 0, BLOCK, lambda d: 3, "arrived")

    def window(recv, index, own_value, reach):
        left = [recv[0, d - 1, index] for d in range(reach, 0, -1)]
        right = [recv[1, d - 1, index] for d in range(1, reach + 1)]
        return jnp.stack(left + [own_value] + right)

    width = 2 * BLOCK + 1
    classes = window(h0_recv, 2, class_f, BLOCK)
    lane = iota((width, 8, LANES), 2)
    row = iota((width, 8, LANES), 1)
    slab = iota((width, 8, LANES), 0) + (me - BLOCK)
    centre = jnp.ones((width, 8, LANES), F32)
    coef = []
    first_last = (
        ((slab == 0) & (row < 4), (slab == n - 1) & (row >= 4)),
        (row % 4 == 0, row % 4 == 3),
        (lane == 0, lane == LANES - 1),
    )
    for direction in range(3):
        speed = pick(
            [vel[k : k + 1, direction : direction + 1] for k in range(kinds)], classes
        )
        if kinds == 1:
            speed = jnp.broadcast_to(speed, (width, 8, LANES))
        forward = jnp.maximum(speed, 0.0)
        backward = jnp.minimum(speed, 0.0)
        centre = centre - (forward - backward)
        coef.append(
            (
                jnp.where(first_last[direction][0], 0.0, forward),
                jnp.where(first_last[direction][1], 0.0, -backward),
            )
        )
    kappa = pick([coup[:, k : k + 1] for k in range(kinds)], classes)
    answers = []
    for i in range(STEPS):
        answers.append(
            kappa
            * pick([powers[k * STEPS + i : k * STEPS + i + 1, 0:1] for k in range(kinds)], classes)
        )

    upper_half = row >= 4

    def advect(u, keep_from, keep_to):
        span = keep_to - keep_from
        pad = jnp.zeros((1, 8, LANES), F32)
        out = []
        part = slice(keep_from, keep_to)
        for m in range(2):
            x = u[m]
            previous = jnp.concatenate([pad, x[: span - 1]], axis=0)
            following = jnp.concatenate([x[1:], pad], axis=0)
            top = upper_half[part]
            low_x = roll_rows(jnp.where(top, previous, x), 4)
            high_x = roll_rows(jnp.where(top, x, following), 4)
            new = centre[part] * x + coef[0][0][part] * low_x + coef[0][1][part] * high_x
            new = new + coef[1][0][part] * roll_rows(x, 1) + coef[1][1][part] * roll_rows(x, 7)
            new = new + coef[2][0][part] * roll_lanes(x, 1) + coef[2][1][part] * roll_lanes(x, -1)
            out.append(new)
        return out

    def response_of(history, lo, hi, now, part):
        first = jnp.zeros((hi - lo, 8, LANES), F32)
        second = jnp.zeros((hi - lo, 8, LANES), F32)
        for at, (start, v0, v1) in history:
            lag = now - at
            a = v0[lo - start : hi - start]
            b = v1[lo - start : hi - start]
            gain = answers[lag][part]
            first = first + gain * a
            second = second + gain * (b + (MEAN_RATE * lag) * a if lag else b)
        return first, second

    def advect_two(u, lo, hi):
        u = advect(u, lo, hi)
        u = advect(u, lo, hi)
        return [x[1:-1] for x in u]

    def block_steps(u, free):
        history = []
        lo, hi = 0, width
        mine = []
        for s in range(BLOCK):
            u = advect_two(u, lo, hi)
            lo, hi = lo + 1, hi - 1
            part = slice(lo, hi)
            v0 = u[0] + TIME_STEP
            v1 = u[1] + MEAN_RATE * u[0]
            history.append((s, (lo, v0, v1)))
            first, second = response_of(history, lo, hi, s, part)
            gain = kappa[part]
            mine.append((v0[BLOCK - lo], v1[BLOCK - lo]))
            u = [
                v0 + gain * (free[s][0] + first - v0),
                v1 + gain * (free[s][1] + second - v1),
            ]
        return u, mine

    def to_cells(half):
        exchange_arrived(tile_send.at[half], tile_recv.at[half], 1 + half)
        slots = jnp.concatenate(to_columns([tile_recv[half, s] for s in range(n)]), axis=1)
        high, low = two_parts(slots)
        cells = half_dot(jnp.concatenate([high, low], axis=0), hot[...])
        cells = cells[:8] + cells[8:]
        for r in range(8):
            fields[r * 8 : (r + 1) * 8] = cells[:, r * LANES : (r + 1) * LANES]
        return [
            (fields[pl.ds(t, 8, stride=8), :], fields[pl.ds(HALF + t, 8, stride=8), :])
            for t in range(HALF)
        ]

    def to_owners(half, mine):
        for t in range(HALF):
            fields[pl.ds(t, 8, stride=8), :] = mine[t][0]
            fields[pl.ds(HALF + t, 8, stride=8), :] = mine[t][1]
        cells = jnp.concatenate([fields[r * 8 : (r + 1) * 8] for r in range(8)], axis=1)
        high, low = two_parts(cells)
        slots = half_dot(jnp.concatenate([high, low], axis=0), hot_t[...])
        for e, block in enumerate(from_columns(split_lanes(slots[:8] + slots[8:]))):
            tile_send[2 + half, e] = block
        exchange_start(tile_send.at[2 + half], tile_recv.at[2 + half], 3 + half)

    early = to_cells(0)
    for t in range(BLOCK - 1):
        h1_send[2 * t] = early[t][0]
        h1_send[2 * t + 1] = early[t][1]
    halo_each(h1_send, h1_recv, 1, BLOCK - 1, lambda d: 2 * (BLOCK - d), "start")
    late = to_cells(1)
    halo_each(h1_send, h1_recv, 1, BLOCK - 1, lambda d: 2 * (BLOCK - d), "arrived")
    moments = [window(h0_recv, m, frac[m], BLOCK) for m in range(2)]
    free = [
        [window(h1_recv, 2 * s + m, early[s][m], BLOCK - 1 - s) for m in range(2)]
        for s in range(BLOCK)
    ]
    moments, mine = block_steps(moments, free)

    own_part = slice(BLOCK, BLOCK + 1)
    h2_send[0] = moments[0][0]
    h2_send[1] = moments[1][0]
    late_free = []
    for t in range(HALF):
        past = [(s, (BLOCK, mine[s][0][None], mine[s][1][None])) for s in range(HALF)]
        first, second = response_of(past, BLOCK, BLOCK + 1, HALF + t, own_part)
        late_free.append((late[t][0] + first[0], late[t][1] + second[0]))
        if t < BLOCK - 1:
            h2_send[2 + 2 * t] = late_free[t][0]
            h2_send[3 + 2 * t] = late_free[t][1]
    halo_each(h2_send, h2_recv, 2, BLOCK, lambda d: 2 + 2 * (BLOCK - d), "start")
    to_owners(0, mine)
    halo_each(h2_send, h2_recv, 2, BLOCK, lambda d: 2 + 2 * (BLOCK - d), "arrived")
    moments = [window(h2_recv, m, moments[m][0], BLOCK) for m in range(2)]
    free = [
        [window(h2_recv, 2 + 2 * s + m, late_free[s][m], BLOCK - 1 - s) for m in range(2)]
        for s in range(BLOCK)
    ]
    moments, mine = block_steps(moments, free)
    to_owners(1, mine)
    age_out[0] = moments[0][0]
    age_out[1] = moments[1][0]

    exchange_arrived(tile_send.at[2], tile_recv.at[2], 3)
    exchange_arrived(tile_send.at[3], tile_recv.at[3], 4)
    first_values = to_columns([tile_recv[2, s] for s in range(n)])
    last_values = to_columns([tile_recv[3, s] for s in range(n)])
    for c in range(chunks):
        pack_out[0, c] = first_values[c]
        pack_out[1, c] = last_values[c]
        pack_out[2, c] = column_class[c]
    store.wait()

    exchange_sent(cls_send, cls_recv, 0)
    for which in range(4):
        exchange_sent(tile_send.at[which], tile_recv.at[which], 1 + which)
    halo_each(h0_send, h0_recv, 0, BLOCK, lambda d: 3, "sent")
    halo_each(h1_send, h1_recv, 1, BLOCK - 1, lambda d: 2 * (BLOCK - d), "sent")
    halo_each(h2_send, h2_recv, 2, BLOCK, lambda d: 2 + 2 * (BLOCK - d), "sent")


def shards(fracture, cell_class, owner, matrix, velocity, coupling, operators):
    n = lax.axis_size("gx")
    nodes, _, slots = matrix.shape
    cap = slots // n
    kinds = operators.shape[0]
    chunks = slots // LANES
    tiled = Layout((0, 2, 1, 3))
    flat = with_layout_constraint(matrix.reshape(nodes, 2, chunks, LANES), tiled)
    flat = flat.transpose(0, 2, 1, 3)
    flat = flat.reshape(nodes * chunks * 2, LANES)
    vmem = pl.BlockSpec(memory_space=pltpu.VMEM)
    anywhere = pl.BlockSpec(memory_space=pl.ANY)
    tall = 2 + 2 * (BLOCK - 1)
    coupling = coupling.reshape(1, kinds)
    age, main, pack, response = pl.pallas_call(
        functools.partial(kernel, n, cap, kinds, chunks),
        out_shape=(
            jax.ShapeDtypeStruct((2, 8, LANES), F32),
            jax.ShapeDtypeStruct(flat.shape, F32),
            jax.ShapeDtypeStruct((3, chunks, 8, LANES), F32),
            jax.ShapeDtypeStruct((nodes, LANES), F32),
        ),
        in_specs=[anywhere] * 7,
        out_specs=(vmem, anywhere, vmem, vmem),
        scratch_shapes=[
            pltpu.VMEM((slots, 8 * LANES), BF16),
            pltpu.VMEM((8 * LANES, slots), BF16),
            pltpu.VMEM(flat.shape, F32),
            pltpu.VMEM((nodes, 2 * slots), BF16),
            pltpu.VMEM((nodes, 2 * slots), BF16),
            pltpu.VMEM(flat.shape, F32),
            pltpu.VMEM((kinds * STEPS, nodes), F32),
            pltpu.VMEM((2 * STEPS, nodes), F32),
            pltpu.VMEM((LANES, nodes), F32),
            pltpu.VMEM((64, LANES), F32),
            pltpu.VMEM((n, 1, LANES), F32),
            pltpu.VMEM((n, 1, LANES), F32),
            pltpu.VMEM((4, n, 8, LANES), F32),
            pltpu.VMEM((4, n, 8, LANES), F32),
            pltpu.VMEM((3, 8, LANES), F32),
            pltpu.VMEM((2, BLOCK, 3, 8, LANES), F32),
            pltpu.VMEM((tall - 2, 8, LANES), F32),
            pltpu.VMEM((2, BLOCK - 1, tall - 2, 8, LANES), F32),
            pltpu.VMEM((tall, 8, LANES), F32),
            pltpu.VMEM((2, BLOCK, tall, 8, LANES), F32),
            pltpu.VMEM((2, 8, LANES), F32),
            pltpu.VMEM((8, LANES), jnp.int32),
            pltpu.VMEM((8, LANES), jnp.int32),
            pltpu.VMEM(velocity.shape, F32),
            pltpu.VMEM((1, kinds), F32),
            pltpu.VMEM(operators.shape, F32),
            pltpu.SemaphoreType.DMA((7,)),
            pltpu.SemaphoreType.DMA,
            pltpu.SemaphoreType.DMA((5, n)),
            pltpu.SemaphoreType.DMA((5, n)),
            pltpu.SemaphoreType.DMA((3, 2, BLOCK)),
            pltpu.SemaphoreType.DMA((3, 2, BLOCK)),
        ],
        compiler_params=pltpu.CompilerParams(
            collective_id=0, has_side_effects=True, vmem_limit_bytes=VMEM_BYTES
        ),
        cost_estimate=pl.CostEstimate(
            flops=2 * 400 * nodes * 2 * slots, bytes_accessed=8 * 2 * nodes * slots, transcendentals=0
        ),
    )(
        fracture.reshape(2, 8, LANES),
        cell_class.reshape(8, LANES),
        owner.reshape(8, LANES),
        flat,
        velocity,
        coupling,
        operators,
    )
    age, out = pl.pallas_call(
        functools.partial(finish, kinds, chunks),
        out_shape=(
            jax.ShapeDtypeStruct((2, 8, LANES), F32),
            jax.ShapeDtypeStruct(flat.shape, F32),
        ),
        in_specs=[anywhere] * 5,
        out_specs=(anywhere, anywhere),
        scratch_shapes=[
            pltpu.VMEM((2, 8, LANES), F32),
            pltpu.VMEM(flat.shape, F32),
            pltpu.VMEM(pack.shape, F32),
            pltpu.VMEM(response.shape, F32),
            pltpu.VMEM((1, kinds), F32),
            pltpu.VMEM((nodes, 2 * slots), F32),
            pltpu.SemaphoreType.DMA((8,)),
            pltpu.SemaphoreType.DMA((5,)),
        ],
        compiler_params=pltpu.CompilerParams(vmem_limit_bytes=VMEM_BYTES),
    )(age, main, pack, response, coupling)
    out = out.reshape(nodes, chunks, 2, LANES).transpose(0, 2, 1, 3)
    out = with_layout_constraint(out, tiled).reshape(matrix.shape)
    return age.reshape(fracture.shape), out


def solution(mesh):
    in_specs = (
        P(None, ("groups", "gx"), None, None),
        P(("groups", "gx"), None, None),
        P(("groups", "gx"), None, None, None),
        P(None, None, ("groups", "gx")),
        P(),
        P(),
        P(),
    )
    out_specs = (P(None, ("groups", "gx"), None, None), P(None, None, ("groups", "gx")))
    return jax.shard_map(shards, mesh=mesh, in_specs=in_specs, out_specs=out_specs, check_vma=False)
```

```python
import functools

import jax
import jax.numpy as jnp
from jax import lax
from jax.experimental import pallas as pl
from jax.experimental.layout import Layout, with_layout_constraint
from jax.experimental.pallas import tpu as pltpu
from jax.sharding import PartitionSpec as P

STEPS = 8
SUBSTEPS = 2
TIME_STEP = 0.125
MEAN_RATE = 2.0 * TIME_STEP
BLOCK = 4
LANES = 128
VMEM_BYTES = 63 * 1024 * 1024
HALF = STEPS // 2

F32 = jnp.float32
BF16 = jnp.bfloat16
NN = (((1,), (0,)), ((), ()))
NT = (((1,), (1,)), ((), ()))


def full_dot(a, b, dims=NN):
    return lax.dot_general(a, b, dims, precision=lax.Precision.HIGHEST, preferred_element_type=F32)


def half_dot(a, b, dims=NN):
    return lax.dot_general(a, b, dims, preferred_element_type=F32)


def two_parts(x):
    high = x.astype(BF16)
    low = (x - high.astype(F32)).astype(BF16)
    return high, low


def iota(shape, dim):
    return lax.broadcasted_iota(jnp.int32, shape, dim)


def roll_rows(x, shift):
    return pltpu.roll(x, shift, x.ndim - 2)


def roll_lanes(x, shift):
    shift = shift % LANES
    return x if shift == 0 else pltpu.roll(x, shift, x.ndim - 1)


def pick(options, which):
    value = options[0]
    for k in range(1, len(options)):
        value = jnp.where(which == float(k), options[k], value)
    return value


def finish(
    kinds,
    chunks,
    age_any,
    main_any,
    pack_any,
    response_any,
    coup_any,
    age_out,
    mat_out,
    age_v,
    main_v,
    pack,
    response_v,
    coup,
    added,
    load_sem,
    store_sem,
):
    nodes = response_any.shape[0]
    stride = 2 * chunks
    bands = 4
    band = nodes // bands
    rows = band * stride

    def band_rows(i):
        return pl.ds(i * rows, rows)

    pairs = [(pack_any, pack), (response_any, response_v), (coup_any, coup), (age_any, age_v)]
    pairs += [(main_any.at[band_rows(i)], main_v.at[band_rows(i)]) for i in range(bands)]
    loads = [
        pltpu.make_async_copy(source, target, load_sem.at[i])
        for i, (source, target) in enumerate(pairs)
    ]
    for load in loads:
        load.start()
    for load in loads[:4]:
        load.wait()
    age_store = pltpu.make_async_copy(age_v, age_out, store_sem.at[bands])
    age_store.start()
    row8 = iota((8, LANES), 0)
    wide_rows = kinds * 16
    remaining = MEAN_RATE * (STEPS - 1 - row8).astype(F32)
    rest = jnp.zeros((LANES - 3 * wide_rows, LANES), BF16)
    right = []
    for c in range(chunks):
        a, b, which = pack[0, c], pack[1, c], pack[2, c]
        v0 = jnp.where(row8 < HALF, a, roll_rows(b, HALF))
        v1 = jnp.where(row8 < HALF, roll_rows(a, HALF), b)
        v1 = v1 + remaining * v0
        for m, value in ((0, v0), (1, v1)):
            pieces = []
            for k in range(kinds):
                belongs = which == float(k)
                pieces.append(jnp.where(belongs, coup[:, k : k + 1] * value, 0.0))
                pieces.append(jnp.where(belongs & (row8 == m), 1.0, 0.0))
            high, low = two_parts(jnp.concatenate(pieces, axis=0))
            right.append(jnp.concatenate([high, low, high, rest], axis=0))
    added[...] = half_dot(response_v[...].astype(BF16), jnp.concatenate(right, axis=1))
    stores = []
    for i in range(bands):
        loads[4 + i].wait()
        for at in range(stride):
            where = pl.ds(i * rows + at, band, stride=stride)
            more = added[i * band : (i + 1) * band, at * LANES : (at + 1) * LANES]
            main_v[where, :] = main_v[where, :] + more
        store = pltpu.make_async_copy(
            main_v.at[band_rows(i)], mat_out.at[band_rows(i)], store_sem.at[i]
        )
        store.start()
        stores.append(store)
    for store in stores:
        store.wait()
    age_store.wait()


def kernel(
    n,
    cap,
    kinds,
    chunks,
    frac_any,
    cls_any,
    own_any,
    mat,
    vel_any,
    coup_any,
    ops_any,
    age_out,
    main_any,
    pack_out,
    response_out,
    hot,
    hot_t,
    mat_v,
    s_hi,
    s_lo,
    main,
    rows_pow,
    cols_pow,
    cols_t,
    fields,
    cls_send,
    cls_recv,
    tile_send,
    tile_recv,
    h0_send,
    h0_recv,
    h1_send,
    h1_recv,
    h2_send,
    h2_recv,
    frac,
    cls,
    own,
    vel,
    coup,
    ops,
    load_sem,
    store_sem,
    a_send_sem,
    a_recv_sem,
    h_send_sem,
    h_recv_sem,
):
    me = lax.axis_index("gx")
    row8 = iota((8, LANES), 0)
    lane8 = iota((8, LANES), 1)

    loads = [
        pltpu.make_async_copy(source, target, load_sem.at[i])
        for i, (source, target) in enumerate(
            (
                (own_any, own),
                (cls_any, cls),
                (frac_any, frac),
                (ops_any, ops),
                (mat, mat_v),
                (vel_any, vel),
                (coup_any, coup),
            )
        )
    ]
    for load in loads:
        load.start()

    sides = ((0, -1), (1, 1))
    for d in range(1, BLOCK + 1):
        for side, sign in sides:
            source = me + sign * d

            @pl.when((source < 0) | (source >= n))
            def _():
                h0_recv[side, d - 1] = jnp.zeros(h0_recv.shape[2:], F32)
                h2_recv[side, d - 1] = jnp.zeros(h2_recv.shape[2:], F32)
                if d < BLOCK:
                    h1_recv[side, d - 1] = jnp.zeros(h1_recv.shape[2:], F32)

    barrier = pltpu.get_barrier_semaphore()

    @pl.loop(1, n)
    def _(d):
        pl.semaphore_signal(
            barrier,
            inc=1,
            device_id={"gx": lax.rem(me + d, n)},
            device_id_type=pl.DeviceIdType.MESH,
        )

    def exchange(send, recv, which, d, peer, landing):
        return pltpu.make_async_remote_copy(
            src_ref=send.at[peer],
            dst_ref=recv.at[landing],
            send_sem=a_send_sem.at[which, d],
            recv_sem=a_recv_sem.at[which, landing],
            device_id={"gx": peer},
            device_id_type=pl.DeviceIdType.MESH,
        )

    def exchange_start(send, recv, which):
        @pl.loop(1, n)
        def _(d):
            exchange(send, recv, which, d, lax.rem(me + d, n), me).start()

        recv[me] = send[me]

    def exchange_arrived(send, recv, which):
        @pl.loop(1, n)
        def _(d):
            source = lax.rem(me + n - d, n)
            exchange(send, recv, which, d, source, source).wait_recv()

    def exchange_sent(send, recv, which):
        @pl.loop(1, n)
        def _(d):
            exchange(send, recv, which, d, lax.rem(me + d, n), me).wait_send()

    def halo(send, recv, which, d, side, sign, rows):
        return pltpu.make_async_remote_copy(
            src_ref=send.at[pl.ds(0, rows)],
            dst_ref=recv.at[side, d - 1, pl.ds(0, rows)],
            send_sem=h_send_sem.at[which, side, d - 1],
            recv_sem=h_recv_sem.at[which, side, d - 1],
            device_id={"gx": me - sign * d},
            device_id_type=pl.DeviceIdType.MESH,
        )

    def halo_each(send, recv, which, reach, rows_of, what):
        for d in range(1, reach + 1):
            for side, sign in sides:
                peer = me + sign * d if what == "arrived" else me - sign * d

                @pl.when((peer >= 0) & (peer < n))
                def _():
                    copy = halo(send, recv, which, d, side, sign, rows_of(d))
                    if what == "start":
                        copy.start()
                    elif what == "arrived":
                        copy.wait_recv()
                    else:
                        copy.wait_send()

    loads[0].wait()
    loads[1].wait()
    owner_f = own[...].astype(F32)
    class_f = cls[...].astype(F32)
    owner_row = iota((n, LANES), 0).astype(F32)
    named = [jnp.where(owner_row == owner_f[r : r + 1, :], 1.0, 0.0) for r in range(8)]
    named_all = jnp.concatenate(named, axis=0).astype(BF16)
    earlier = jnp.where(iota((LANES, LANES), 0) < iota((LANES, LANES), 1), 1.0, 0.0).astype(BF16)
    before = half_dot(named_all, earlier)
    total = half_dot(named_all, jnp.ones((LANES, LANES), BF16))
    base = jnp.zeros((n, LANES), F32)
    places = []
    for r in range(8):
        count = before[r * n : (r + 1) * n] + base
        base = base + total[r * n : (r + 1) * n]
        arrival = jnp.sum(named[r] * count, axis=0, keepdims=True)
        places.append(owner_f[r : r + 1, :] * float(cap) + arrival)
    slot_lane = iota((LANES, LANES), 1).astype(F32)
    for r in range(8):
        place = jnp.broadcast_to(places[r], (LANES, LANES)).T
        for c in range(chunks):
            hit = slot_lane == (place - float(c * LANES))
            hot_t[r * LANES : (r + 1) * LANES, c * LANES : (c + 1) * LANES] = jnp.where(
                hit, 1.0, 0.0
            ).astype(BF16)

    def to_columns(blocks):
        out = [jnp.zeros((8, LANES), F32) for _ in range(chunks)]
        for s in range(n):
            at, off = divmod(s * cap, LANES)
            turned = roll_lanes(blocks[s], off)
            if off + cap <= LANES:
                out[at] = out[at] + turned
            else:
                out[at] = out[at] + jnp.where(lane8 >= off, turned, 0.0)
                out[at + 1] = out[at + 1] + jnp.where(lane8 < off, turned, 0.0)
        return out

    def from_columns(columns):
        out = []
        for s in range(n):
            at, off = divmod(s * cap, LANES)
            block = roll_lanes(columns[at], -off)
            if off + cap > LANES:
                block = jnp.where(lane8 < LANES - off, block, roll_lanes(columns[at + 1], -off))
            out.append(jnp.where(lane8 < cap, block, 0.0))
        return out

    def split_lanes(x):
        return [x[:, c * LANES : (c + 1) * LANES] for c in range(chunks)]

    class_rows = jnp.concatenate(
        [jnp.broadcast_to(class_f[r : r + 1, :], (16, LANES)) for r in range(8)], axis=1
    ).astype(BF16)
    class_out = half_dot(class_rows, hot_t[...])
    for e, block in enumerate(from_columns(split_lanes(class_out[:8]))):
        cls_send[e] = block[0:1]
    loads[2].wait()
    h0_send[0] = frac[0]
    h0_send[1] = frac[1]
    h0_send[2] = class_f

    pl.semaphore_wait(barrier, n - 1)
    exchange_start(cls_send, cls_recv, 0)
    halo_each(h0_send, h0_recv, 0, BLOCK, lambda d: 3, "start")

    slot_row = iota((LANES, LANES), 0).astype(F32)
    for c in range(chunks):
        for r in range(8):
            hit = slot_row == (places[r] - float(c * LANES))
            hot[c * LANES : (c + 1) * LANES, r * LANES : (r + 1) * LANES] = jnp.where(
                hit, 1.0, 0.0
            ).astype(BF16)

    loads[3].wait()
    rows_pow[...] = jnp.zeros(rows_pow.shape, F32)
    squares, fourths = [], []
    for k in range(kinds):
        first = ops[k]
        square = full_dot(first, first)
        fourth = full_dot(square, square)
        squares.append(square)
        fourths.append(fourth)
        at = k * STEPS
        rows_pow[at : at + 1] = first[0:1]
        rows_pow[at + 1 : at + 2] = square[0:1]
        rows_pow[at + 2 : at + 4] = full_dot(rows_pow[at : at + 8], square)[0:2]
        rows_pow[at + 4 : at + 8] = full_dot(rows_pow[at : at + 8], fourth)[0:4]

    for load in loads[4:]:
        load.wait()
    stride = 2 * chunks
    for m in range(2):
        for c in range(chunks):
            at = (m * chunks + c) * LANES
            block = mat_v[pl.ds(c * 2 + m, LANES, stride=stride), :]
            high, low = two_parts(block)
            s_hi[:, at : at + LANES] = high
            s_lo[:, at : at + LANES] = low

    powers = rows_pow[...]
    p_high, p_low = two_parts(powers)
    wide = half_dot(jnp.concatenate([p_high, p_low], axis=0), s_hi[...])
    count = kinds * STEPS
    q_all = wide[:count] + wide[count:] + half_dot(p_high, s_lo[...])

    exchange_arrived(cls_send, cls_recv, 0)

    column_class = to_columns([jnp.broadcast_to(cls_recv[s], (8, LANES)) for s in range(n)])

    steady0, steady1 = [], []
    for k in range(kinds):
        sums = jnp.sum(powers[k * STEPS : (k + 1) * STEPS], axis=1, keepdims=True)
        sums = jnp.broadcast_to(sums, (STEPS, LANES))
        zero_sum = jnp.zeros((STEPS, LANES), F32)
        one_sum = jnp.zeros((STEPS, LANES), F32)
        for i in range(STEPS):
            term = jnp.where(row8 >= i, sums[i : i + 1], 0.0)
            zero_sum = zero_sum + TIME_STEP * term
            one_sum = one_sum + (TIME_STEP * MEAN_RATE * i) * term
        steady0.append(zero_sum)
        steady1.append(one_sum)

    step_row = (row8 + 1).astype(F32)
    tiles_a, tiles_b = [], []
    for c in range(chunks):
        parts = []
        for m in range(2):
            at = (m * chunks + c) * LANES
            parts.append(
                pick(
                    [q_all[k * STEPS : (k + 1) * STEPS, at : at + LANES] for k in range(kinds)],
                    column_class[c],
                )
            )
        free0 = parts[0] + pick(steady0, column_class[c])
        free1 = parts[1] + MEAN_RATE * step_row * parts[0] + pick(steady1, column_class[c])
        tiles_a.append(jnp.where(row8 < HALF, free0, roll_rows(free1, HALF)))
        tiles_b.append(jnp.where(row8 < HALF, roll_rows(free0, HALF), free1))
    for half, tiles in ((0, tiles_a), (1, tiles_b)):
        blocks = from_columns(tiles)
        for e in range(n):
            tile_send[half, e] = blocks[e]
    exchange_start(tile_send.at[0], tile_recv.at[0], 1)

    eights = [full_dot(fourths[k], fourths[k]) for k in range(kinds)]
    e_high, e_low = two_parts(jnp.concatenate(eights, axis=0))
    nodes = eights[0].shape[0]
    for b in range(chunks):
        lanes = slice(b * 2 * LANES, (b + 1) * 2 * LANES)
        right = s_hi[:, lanes]
        both = half_dot(e_high, right) + half_dot(e_low, right) + half_dot(e_high, s_lo[:, lanes])
        for i in range(2):
            at = b * 2 + i
            m, c = divmod(at, chunks)
            value = pick(
                [
                    both[k * nodes : (k + 1) * nodes, i * LANES : (i + 1) * LANES]
                    for k in range(kinds)
                ],
                column_class[c][0:1],
            )
            if m == 1:
                mean = main[pl.ds(2 * c, nodes, stride=stride), :]
                value = value + (STEPS * MEAN_RATE) * mean
            main[pl.ds(2 * c + m, nodes, stride=stride), :] = value
    exchange_start(tile_send.at[1], tile_recv.at[1], 2)
    store = pltpu.make_async_copy(main, main_any, store_sem)
    store.start()

    wide_rows = kinds * 16
    cols_t[...] = jnp.zeros(cols_t.shape, F32)
    for k in range(kinds):
        turned = ops[k].T
        cols_pow[...] = jnp.zeros(cols_pow.shape, F32)
        cols_pow[0:1] = turned[0:1]
        cols_pow[1:2] = jnp.sum(turned, axis=0, keepdims=True)
        cols_pow[2:4] = full_dot(cols_pow[0:8], ops[k], NT)[0:2]
        cols_pow[4:8] = full_dot(cols_pow[0:8], squares[k], NT)[0:4]
        cols_pow[8:16] = full_dot(cols_pow[0:8], fourths[k], NT)
        zero_sum = jnp.zeros((1, LANES), F32)
        one_sum = jnp.zeros((1, LANES), F32)
        for i in range(STEPS):
            cols_t[k * 16 + 7 - i : k * 16 + 8 - i] = cols_pow[2 * i : 2 * i + 1]
            source_row = cols_pow[2 * i + 1 : 2 * i + 2]
            zero_sum = zero_sum + TIME_STEP * source_row
            one_sum = one_sum + (TIME_STEP * MEAN_RATE * i) * source_row
        cols_t[k * 16 + 8 : k * 16 + 9] = zero_sum
        cols_t[k * 16 + 9 : k * 16 + 10] = one_sum
    whole = cols_t[0:wide_rows]
    whole_high = whole.astype(BF16).astype(F32)
    cols_t[0:wide_rows] = whole_high
    cols_t[wide_rows : 2 * wide_rows] = whole_high
    cols_t[2 * wide_rows : 3 * wide_rows] = whole - whole_high
    response_out[...] = cols_t[...].T

    halo_each(h0_send, h0_recv, 0, BLOCK, lambda d: 3, "arrived")

    def window(recv, index, own_value, reach):
        left = [recv[0, d - 1, index] for d in range(reach, 0, -1)]
        right = [recv[1, d - 1, index] for d in range(1, reach + 1)]
        return jnp.stack(left + [own_value] + right)

    width = 2 * BLOCK + 1
    classes = window(h0_recv, 2, class_f, BLOCK)
    lane = iota((width, 8, LANES), 2)
    row = iota((width, 8, LANES), 1)
    slab = iota((width, 8, LANES), 0) + (me - BLOCK)
    centre = jnp.ones((width, 8, LANES), F32)
    coef = []
    first_last = (
        ((slab == 0) & (row < 4), (slab == n - 1) & (row >= 4)),
        (row % 4 == 0, row % 4 == 3),
        (lane == 0, lane == LANES - 1),
    )
    for direction in range(3):
        speed = pick(
            [vel[k : k + 1, direction : direction + 1] for k in range(kinds)], classes
        )
        if kinds == 1:
            speed = jnp.broadcast_to(speed, (width, 8, LANES))
        forward = jnp.maximum(speed, 0.0)
        backward = jnp.minimum(speed, 0.0)
        centre = centre - (forward - backward)
        coef.append(
            (
                jnp.where(first_last[direction][0], 0.0, forward),
                jnp.where(first_last[direction][1], 0.0, -backward),
            )
        )
    kappa = pick([coup[:, k : k + 1] for k in range(kinds)], classes)
    answers = []
    for i in range(STEPS):
        answers.append(
            kappa
            * pick([powers[k * STEPS + i : k * STEPS + i + 1, 0:1] for k in range(kinds)], classes)
        )

    upper_half = row >= 4

    def advect(u, keep_from, keep_to):
        span = keep_to - keep_from
        pad = jnp.zeros((1, 8, LANES), F32)
        out = []
        part = slice(keep_from, keep_to)
        for m in range(2):
            x = u[m]
            previous = jnp.concatenate([pad, x[: span - 1]], axis=0)
            following = jnp.concatenate([x[1:], pad], axis=0)
            top = upper_half[part]
            low_x = roll_rows(jnp.where(top, previous, x), 4)
            high_x = roll_rows(jnp.where(top, x, following), 4)
            new = centre[part] * x + coef[0][0][part] * low_x + coef[0][1][part] * high_x
            new = new + coef[1][0][part] * roll_rows(x, 1) + coef[1][1][part] * roll_rows(x, 7)
            new = new + coef[2][0][part] * roll_lanes(x, 1) + coef[2][1][part] * roll_lanes(x, -1)
            out.append(new)
        return out

    def response_of(history, lo, hi, now, part):
        first = jnp.zeros((hi - lo, 8, LANES), F32)
        second = jnp.zeros((hi - lo, 8, LANES), F32)
        for at, (start, v0, v1) in history:
            lag = now - at
            a = v0[lo - start : hi - start]
            b = v1[lo - start : hi - start]
            gain = answers[lag][part]
            first = first + gain * a
            second = second + gain * (b + (MEAN_RATE * lag) * a if lag else b)
        return first, second

    def advect_two(u, lo, hi):
        u = advect(u, lo, hi)
        u = advect(u, lo, hi)
        return [x[1:-1] for x in u]

    def block_steps(u, free):
        history = []
        lo, hi = 0, width
        mine = []
        for s in range(BLOCK):
            u = advect_two(u, lo, hi)
            lo, hi = lo + 1, hi - 1
            part = slice(lo, hi)
            v0 = u[0] + TIME_STEP
            v1 = u[1] + MEAN_RATE * u[0]
            history.append((s, (lo, v0, v1)))
            first, second = response_of(history, lo, hi, s, part)
            gain = kappa[part]
            mine.append((v0[BLOCK - lo], v1[BLOCK - lo]))
            u = [
                v0 + gain * (free[s][0] + first - v0),
                v1 + gain * (free[s][1] + second - v1),
            ]
        return u, mine

    def to_cells(half):
        exchange_arrived(tile_send.at[half], tile_recv.at[half], 1 + half)
        slots = jnp.concatenate(to_columns([tile_recv[half, s] for s in range(n)]), axis=1)
        high, low = two_parts(slots)
        cells = half_dot(jnp.concatenate([high, low], axis=0), hot[...])
        cells = cells[:8] + cells[8:]
        for r in range(8):
            fields[r * 8 : (r + 1) * 8] = cells[:, r * LANES : (r + 1) * LANES]
        return [
            (fields[pl.ds(t, 8, stride=8), :], fields[pl.ds(HALF + t, 8, stride=8), :])
            for t in range(HALF)
        ]

    def to_owners(half, mine):
        for t in range(HALF):
            fields[pl.ds(t, 8, stride=8), :] = mine[t][0]
            fields[pl.ds(HALF + t, 8, stride=8), :] = mine[t][1]
        cells = jnp.concatenate([fields[r * 8 : (r + 1) * 8] for r in range(8)], axis=1)
        high, low = two_parts(cells)
        slots = half_dot(jnp.concatenate([high, low], axis=0), hot_t[...])
        for e, block in enumerate(from_columns(split_lanes(slots[:8] + slots[8:]))):
            tile_send[2 + half, e] = block
        exchange_start(tile_send.at[2 + half], tile_recv.at[2 + half], 3 + half)

    early = to_cells(0)
    for t in range(BLOCK - 1):
        h1_send[2 * t] = early[t][0]
        h1_send[2 * t + 1] = early[t][1]
    halo_each(h1_send, h1_recv, 1, BLOCK - 1, lambda d: 2 * (BLOCK - d), "start")
    late = to_cells(1)
    halo_each(h1_send, h1_recv, 1, BLOCK - 1, lambda d: 2 * (BLOCK - d), "arrived")
    moments = [window(h0_recv, m, frac[m], BLOCK) for m in range(2)]
    free = [
        [window(h1_recv, 2 * s + m, early[s][m], BLOCK - 1 - s) for m in range(2)]
        for s in range(BLOCK)
    ]
    moments, mine = block_steps(moments, free)

    own_part = slice(BLOCK, BLOCK + 1)
    h2_send[0] = moments[0][0]
    h2_send[1] = moments[1][0]
    late_free = []
    for t in range(HALF):
        past = [(s, (BLOCK, mine[s][0][None], mine[s][1][None])) for s in range(HALF)]
        first, second = response_of(past, BLOCK, BLOCK + 1, HALF + t, own_part)
        late_free.append((late[t][0] + first[0], late[t][1] + second[0]))
        if t < BLOCK - 1:
            h2_send[2 + 2 * t] = late_free[t][0]
            h2_send[3 + 2 * t] = late_free[t][1]
    halo_each(h2_send, h2_recv, 2, BLOCK, lambda d: 2 + 2 * (BLOCK - d), "start")
    to_owners(0, mine)
    halo_each(h2_send, h2_recv, 2, BLOCK, lambda d: 2 + 2 * (BLOCK - d), "arrived")
    moments = [window(h2_recv, m, moments[m][0], BLOCK) for m in range(2)]
    free = [
        [window(h2_recv, 2 + 2 * s + m, late_free[s][m], BLOCK - 1 - s) for m in range(2)]
        for s in range(BLOCK)
    ]
    moments, mine = block_steps(moments, free)
    to_owners(1, mine)
    age_out[0] = moments[0][0]
    age_out[1] = moments[1][0]

    exchange_arrived(tile_send.at[2], tile_recv.at[2], 3)
    exchange_arrived(tile_send.at[3], tile_recv.at[3], 4)
    first_values = to_columns([tile_recv[2, s] for s in range(n)])
    last_values = to_columns([tile_recv[3, s] for s in range(n)])
    for c in range(chunks):
        pack_out[0, c] = first_values[c]
        pack_out[1, c] = last_values[c]
        pack_out[2, c] = column_class[c]
    store.wait()

    exchange_sent(cls_send, cls_recv, 0)
    for which in range(4):
        exchange_sent(tile_send.at[which], tile_recv.at[which], 1 + which)
    halo_each(h0_send, h0_recv, 0, BLOCK, lambda d: 3, "sent")
    halo_each(h1_send, h1_recv, 1, BLOCK - 1, lambda d: 2 * (BLOCK - d), "sent")
    halo_each(h2_send, h2_recv, 2, BLOCK, lambda d: 2 + 2 * (BLOCK - d), "sent")


def shards(fracture, cell_class, owner, matrix, velocity, coupling, operators):
    n = lax.axis_size("gx")
    nodes, _, slots = matrix.shape
    cap = slots // n
    kinds = operators.shape[0]
    chunks = slots // LANES
    tiled = Layout((0, 2, 1, 3))
    flat = with_layout_constraint(matrix.reshape(nodes, 2, chunks, LANES), tiled)
    flat = flat.transpose(0, 2, 1, 3)
    flat = flat.reshape(nodes * chunks * 2, LANES)
    vmem = pl.BlockSpec(memory_space=pltpu.VMEM)
    anywhere = pl.BlockSpec(memory_space=pl.ANY)
    tall = 2 + 2 * (BLOCK - 1)
    coupling = coupling.reshape(1, kinds)
    age, main, pack, response = pl.pallas_call(
        functools.partial(kernel, n, cap, kinds, chunks),
        out_shape=(
            jax.ShapeDtypeStruct((2, 8, LANES), F32),
            jax.ShapeDtypeStruct(flat.shape, F32),
            jax.ShapeDtypeStruct((3, chunks, 8, LANES), F32),
            jax.ShapeDtypeStruct((nodes, LANES), F32),
        ),
        in_specs=[anywhere] * 7,
        out_specs=(vmem, anywhere, vmem, vmem),
        scratch_shapes=[
            pltpu.VMEM((slots, 8 * LANES), BF16),
            pltpu.VMEM((8 * LANES, slots), BF16),
            pltpu.VMEM(flat.shape, F32),
            pltpu.VMEM((nodes, 2 * slots), BF16),
            pltpu.VMEM((nodes, 2 * slots), BF16),
            pltpu.VMEM(flat.shape, F32),
            pltpu.VMEM((kinds * STEPS, nodes), F32),
            pltpu.VMEM((2 * STEPS, nodes), F32),
            pltpu.VMEM((LANES, nodes), F32),
            pltpu.VMEM((64, LANES), F32),
            pltpu.VMEM((n, 1, LANES), F32),
            pltpu.VMEM((n, 1, LANES), F32),
            pltpu.VMEM((4, n, 8, LANES), F32),
            pltpu.VMEM((4, n, 8, LANES), F32),
            pltpu.VMEM((3, 8, LANES), F32),
            pltpu.VMEM((2, BLOCK, 3, 8, LANES), F32),
            pltpu.VMEM((tall - 2, 8, LANES), F32),
            pltpu.VMEM((2, BLOCK - 1, tall - 2, 8, LANES), F32),
            pltpu.VMEM((tall, 8, LANES), F32),
            pltpu.VMEM((2, BLOCK, tall, 8, LANES), F32),
            pltpu.VMEM((2, 8, LANES), F32),
            pltpu.VMEM((8, LANES), jnp.int32),
            pltpu.VMEM((8, LANES), jnp.int32),
            pltpu.VMEM(velocity.shape, F32),
            pltpu.VMEM((1, kinds), F32),
            pltpu.VMEM(operators.shape, F32),
            pltpu.SemaphoreType.DMA((7,)),
            pltpu.SemaphoreType.DMA,
            pltpu.SemaphoreType.DMA((5, n)),
            pltpu.SemaphoreType.DMA((5, n)),
            pltpu.SemaphoreType.DMA((3, 2, BLOCK)),
            pltpu.SemaphoreType.DMA((3, 2, BLOCK)),
        ],
        compiler_params=pltpu.CompilerParams(
            collective_id=0, has_side_effects=True, vmem_limit_bytes=VMEM_BYTES
        ),
        cost_estimate=pl.CostEstimate(
            flops=2 * 400 * nodes * 2 * slots, bytes_accessed=8 * 2 * nodes * slots, transcendentals=0
        ),
    )(
        fracture.reshape(2, 8, LANES),
        cell_class.reshape(8, LANES),
        owner.reshape(8, LANES),
        flat,
        velocity,
        coupling,
        operators,
    )
    age, out = pl.pallas_call(
        functools.partial(finish, kinds, chunks),
        out_shape=(
            jax.ShapeDtypeStruct((2, 8, LANES), F32),
            jax.ShapeDtypeStruct(flat.shape, F32),
        ),
        in_specs=[anywhere] * 5,
        out_specs=(anywhere, anywhere),
        scratch_shapes=[
            pltpu.VMEM((2, 8, LANES), F32),
            pltpu.VMEM(flat.shape, F32),
            pltpu.VMEM(pack.shape, F32),
            pltpu.VMEM(response.shape, F32),
            pltpu.VMEM((1, kinds), F32),
            pltpu.VMEM((nodes, 2 * slots), F32),
            pltpu.SemaphoreType.DMA((8,)),
            pltpu.SemaphoreType.DMA((5,)),
        ],
        compiler_params=pltpu.CompilerParams(vmem_limit_bytes=VMEM_BYTES),
    )(age, main, pack, response, coupling)
    out = out.reshape(nodes, chunks, 2, LANES).transpose(0, 2, 1, 3)
    out = with_layout_constraint(out, tiled).reshape(matrix.shape)
    return age.reshape(fracture.shape), out


def solution(mesh):
    in_specs = (
        P(None, ("groups", "gx"), None, None),
        P(("groups", "gx"), None, None),
        P(("groups", "gx"), None, None, None),
        P(None, None, ("groups", "gx")),
        P(),
        P(),
        P(),
    )
    out_specs = (P(None, ("groups", "gx"), None, None), P(None, None, ("groups", "gx")))
    return jax.shard_map(shards, mesh=mesh, in_specs=in_specs, out_specs=out_specs, check_vma=False)
```
